32 devices in a mesh: seq: 4 (over x, core), batch: 8 (over z, y).
Axes of the slice: x: 2, y: 2, z: 4, core: 2. Of those that a mesh axis runs over, the one named last changes fastest.
Arguments:
- tokens: bfloat16 [8, 1024, 2048], P('batch', 'seq'), may hold values from -6 to 6
- decays: float32 [8, 16, 1024], P('batch', None, 'seq'), may hold values from 0.1 to 1
- out_grad: bfloat16 [8, 1024, 2048], P('batch', 'seq'), may hold values from -6 to 6
- mixer_gain: bfloat16 [2048], P(('seq', 'batch')), may hold values from 0.5 to 1.5
- query_weight: bfloat16 [2048, 2048], P(None, ('seq', 'batch')), may hold values from -0.125 to 0.125
- key_weight: bfloat16 [2048, 2048], P(None, ('seq', 'batch')), may hold values from -0.125 to 0.125
- value_weight: bfloat16 [2048, 4096], P(None, ('seq', 'batch')), may hold values from -0.125 to 0.125
- beta_weight: bfloat16 [2048, 16], P(('seq', 'batch')), may hold values from -0.25 to 0.25
- outgate_weight: bfloat16 [2048, 4096], P(None, ('seq', 'batch')), may hold values from -0.125 to 0.125
- query_conv: bfloat16 [4, 2048], P(None, ('seq', 'batch')), may hold values from -3 to 3
- key_conv: bfloat16 [4, 2048], P(None, ('seq', 'batch')), may hold values from -3 to 3
- value_conv: bfloat16 [4, 4096], P(None, ('seq', 'batch')), may hold values from -3 to 3
- head_gain: bfloat16 [256], P(('seq', 'batch')), may hold values from 0.5 to 1.5
- output_weight: bfloat16 [4096, 2048], P(('seq', 'batch')), may hold values from -0.125 to 0.125
- feed_gain: bfloat16 [2048], P(('seq', 'batch')), may hold values from 0.5 to 1.5
- feed_gate: bfloat16 [2048, 5632], P(None, ('seq', 'batch')), may hold values from -0.125 to 0.125
- feed_up: bfloat16 [2048, 5632], P(None, ('seq', 'batch')), may hold values from -0.125 to 0.125
- feed_down: bfloat16 [5632, 2048], P(('seq', 'batch')), may hold values from -0.109375 to 0.109375
Outputs:
- block_out: bfloat16 [8, 1024, 2048], P('batch', 'seq')
- tokens_grad: bfloat16 [8, 1024, 2048], P('batch', 'seq')
- mixer_gain_grad: float32 [2048], P(('seq', 'batch'))
- query_weight_grad: float32 [2048, 2048], P(None, ('seq', 'batch'))
- key_weight_grad: float32 [2048, 2048], P(None, ('seq', 'batch'))
- value_weight_grad: float32 [2048, 4096], P(None, ('seq', 'batch'))
- beta_weight_grad: float32 [2048, 16], P(('seq', 'batch'))
- outgate_weight_grad: float32 [2048, 4096], P(None, ('seq', 'batch'))
- query_conv_grad: float32 [4, 2048], P(None, ('seq', 'batch'))
- key_conv_grad: float32 [4, 2048], P(None, ('seq', 'batch'))
- value_conv_grad: float32 [4, 4096], P(None, ('seq', 'batch'))
- head_gain_grad: float32 [256], P(('seq', 'batch'))
- output_weight_grad: float32 [4096, 2048], P(('seq', 'batch'))
- feed_gain_grad: float32 [2048], P(('seq', 'batch'))
- feed_gate_grad: float32 [2048, 5632], P(None, ('seq', 'batch'))
- feed_up_grad: float32 [2048, 5632], P(None, ('seq', 'batch'))
- descent_projection_adjoint: float32 [5632, 2048], P(('seq', 'batch'))
The draws below stay inside these ranges and needn't reach their ends.
All inputs are finite; a program needn't handle non-finite values.
Results may differ from the reference program's by a relative error of at most 0.024.
Values may be sent and summed in bfloat16 or wider, within the bound.
No kernel may reach another device: no remote copies, remote signals or barrier semaphores. Data moves between devices by JAX's collectives and lax.ppermute only.
A program may use at most 576 MiB of HBM per device.

```python
import math
import jax
import jax.numpy as jnp
from jax import lax

D = 2048
H = 16
DK = 128
DV = 256
FF = 5632
STRETCH = 64
KERNEL = 4
TOK_DEV = 256
KD = 2048
VD = 4096
LENGTH = 1024
SEQS = 8


def draw_decays(key, part):
    key = jax.random.fold_in(key, 7)
    keys = jax.random.split(key, 5)
    span_low = 30.0
    span_high = 4.0 * LENGTH
    spans = jnp.exp(jax.random.uniform(keys[0], (SEQS, H, 1), jnp.float32, math.log(span_low), math.log(span_high)))
    jitter = jnp.exp(jax.random.uniform(keys[1], (SEQS, H, LENGTH), jnp.float32, -0.69, 0.69))
    blocks = LENGTH // TOK_DEV
    device_scale = jnp.exp(jax.random.uniform(keys[2], (SEQS, H, blocks, 1), jnp.float32, -0.69, 0.69))
    device_scale = jnp.broadcast_to(device_scale, (SEQS, H, blocks, TOK_DEV)).reshape(SEQS, H, LENGTH)
    places = jax.random.randint(keys[3], (SEQS, 1, 1, 3), 0, LENGTH)
    positions = lax.broadcasted_iota(jnp.int32, (SEQS, 1, LENGTH, 3), 2)
    strength = jax.random.uniform(keys[4], (SEQS, H, 1, 3), jnp.float32, 0.2, 0.5)
    losses = jnp.sum(jnp.where(positions == places, -jnp.log(1.0 - strength), 0.0), axis=-1)
    rates = jitter * device_scale / spans
    return jnp.exp(-rates - losses)


def strengthened(array, rng, source, target, shards_of, factor):
    def block_of(dim):
        return (jnp.arange(array.shape[dim]) // (array.shape[dim] // shards_of)).reshape((-1,) + (1,) * (array.ndim - 1 - dim))

    one_side = jax.random.permutation(rng, shards_of)[block_of(target)]
    other_side = (block_of(target) + shards_of // 2) % shards_of
    return jnp.where((block_of(source) == one_side) | (block_of(source) == other_side), factor * array, array)


def levels(own_key, extent, shards, smallest, high):
    factor_of = 1.0
    for axis_at, parts in shards:
        steps = jax.random.uniform(jax.random.fold_in(jax.random.fold_in(own_key, 6), axis_at), (parts,), jnp.float32, smallest / len(shards), high / len(shards))
        factor_of = factor_of * jnp.repeat(jnp.exp(steps), extent[axis_at] // parts).reshape((-1,) + (1,) * (len(extent) - 1 - axis_at))
    return factor_of


def centred(rng, extent, deviation, bound, cuts=(), kind=jnp.bfloat16):
    factor_of = levels(rng, extent, cuts, -0.22, 0.18) if cuts else 1.0
    entries = jax.random.normal(rng, extent, jnp.float32) * deviation * factor_of
    return jnp.minimum(jnp.maximum(entries, -bound), bound).astype(kind)


def noise_with(stream_key, dims, width, bound, pieces, heavy, kind=jnp.bfloat16):
    values = width * jax.random.normal(stream_key, dims, jnp.float32)
    if pieces:
        values = values * levels(stream_key, dims, pieces, -0.22, 0.18)
    return jnp.clip(strengthened(values, jax.random.fold_in(stream_key, 3), *heavy), -bound, bound).astype(kind)


def setup_inputs(seed: int = 0) -> dict:
    splits = jax.random.split(jax.random.key(seed), 19)
    return {
        "tokens": noise_with(splits[0], (SEQS, LENGTH, D), 1.0, 6.0, ((0, 8), (1, 4)), (1, 2, 4, 2.0)),
        "decays": draw_decays(jax.random.fold_in(splits[18], 71), 0),
        "out_grad": noise_with(splits[2], (SEQS, LENGTH, D), 1.0, 6.0, ((0, 8), (1, 4)), (1, 2, 4, 2.0)),
        "mixer_gain": jnp.clip(1.0 + 0.1 * jax.random.normal(splits[3], (D,), jnp.float32), 0.5, 1.5).astype(jnp.bfloat16),
        "query_weight": centred(splits[4], (D, KD), D ** -0.5, 0.125, ((1, 32),)),
        "key_weight": centred(splits[5], (D, KD), D ** -0.5, 0.125, ((1, 32),)),
        "value_weight": centred(splits[6], (D, VD), D ** -0.5, 0.125, ((1, 32),)),
        "beta_weight": centred(splits[7], (D, H), (D // 4) ** -0.5, 0.25, ((0, 32),)),
        "outgate_weight": centred(splits[8], (D, VD), D ** -0.5, 0.125, ((1, 32),)),
        "query_conv": centred(splits[9], (KERNEL, KD), KERNEL ** -0.5, 3.0, ((1, 32),)),
        "key_conv": centred(splits[10], (KERNEL, KD), KERNEL ** -0.5, 3.0, ((1, 32),)),
        "value_conv": centred(splits[11], (KERNEL, VD), KERNEL ** -0.5, 3.0, ((1, 32),)),
        "head_gain": jnp.clip(1.0 + 0.1 * jax.random.normal(splits[12], (DV,), jnp.float32), 0.5, 1.5).astype(jnp.bfloat16),
        "output_weight": centred(splits[13], (VD, D), (VD // 2) ** -0.5, 0.125, ((0, 32),)),
        "feed_gain": jnp.clip(1.0 + 0.1 * jax.random.normal(splits[14], (D,), jnp.float32), 0.5, 1.5).astype(jnp.bfloat16),
        "feed_gate": centred(splits[15], (D, FF), D ** -0.5, 0.125, ((1, 32),)),
        "feed_up": centred(splits[16], (D, FF), D ** -0.5, 0.125, ((1, 32),)),
        "feed_down": centred(splits[17], (FF, D), (FF // 2) ** -0.5, 0.109375, ((0, 32),)),
    }


@jax.custom_vjp
def low(v):
    return lax.optimization_barrier(v.astype(jnp.bfloat16)).astype(jnp.float32)

@jax.custom_vjp
def low_back(v):
    return v

def low_keep(v):
    return (low(v), None)

def low_pass(kept, grad):
    return (grad,)

def back_keep(v):
    return (v, None)

def back_low(kept, grad):
    return (low(grad),)
low.defvjp(low_keep, low_pass)
low_back.defvjp(back_keep, back_low)
EPS_NORM = 1e-05
EPS_UNIT = 1e-06
FULL_PRODUCT = lax.Precision.HIGHEST

def matmul(left_side, right_side):
    return jnp.dot(left_side, right_side, precision=FULL_PRODUCT)

def rms_scale(values, gain_vals):
    return values * lax.rsqrt(lax.optimization_barrier(jnp.mean(values * values, axis=-1, keepdims=True)) + EPS_NORM) * gain_vals

def unit_rows(values):
    return values * lax.rsqrt(lax.optimization_barrier(jnp.sum(values * values, axis=-1, keepdims=True)) + EPS_UNIT)

def stretch_parts(queries, key_rows, value_rows, beta_vals, log_decay):
    block_len = log_decay.shape[-1]
    key_width = key_rows.shape[-1]
    totals = jnp.cumsum(log_decay, axis=-1)
    row_index = lax.broadcasted_iota(jnp.int32, (block_len, block_len), 0)
    col_index = lax.broadcasted_iota(jnp.int32, (block_len, block_len), 1)
    lower_mask = row_index >= col_index
    strict_mask = row_index > col_index
    log_gap = totals[..., :, None] - totals[..., None, :]
    decay_ratio = jnp.where(lower_mask, jnp.exp(jnp.where(lower_mask, log_gap, 0.0)), 0.0)
    keys_keys = jnp.einsum('...ck,...dk->...cd', key_rows, key_rows, precision=FULL_PRODUCT)
    query_keys = jnp.einsum('...ck,...dk->...cd', queries, key_rows, precision=FULL_PRODUCT)
    coupling = jnp.where(strict_mask, beta_vals[..., :, None] * decay_ratio * keys_keys, 0.0)
    system = coupling + jnp.eye(block_len, dtype=jnp.float32)
    growth = jnp.exp(totals)
    right_side = jnp.concatenate([(beta_vals * growth)[..., None] * key_rows, beta_vals[..., None] * value_rows], axis=-1)
    solved = jax.scipy.linalg.solve_triangular(system, right_side, lower=True, unit_diagonal=True)
    weight_part = solved[..., :key_width]
    value_part = solved[..., key_width:]
    scores = decay_ratio * query_keys
    shard_local_output = jnp.einsum('...ct,...tv->...cv', scores, value_part, precision=FULL_PRODUCT)
    initial_query = growth[..., None] * queries - jnp.einsum('...ct,...tk->...ck', scores, weight_part, precision=FULL_PRODUCT)
    last_total = totals[..., -1:]
    fadeout = jnp.exp(last_total - totals)
    state_transition = jnp.exp(last_total)[..., None] * jnp.eye(key_width, dtype=jnp.float32) - jnp.einsum('...ck,...cj->...kj', key_rows, fadeout[..., None] * weight_part, precision=FULL_PRODUCT)
    state_increment = jnp.einsum('...ck,...cv->...kv', key_rows, fadeout[..., None] * value_part, precision=FULL_PRODUCT)
    return (shard_local_output, initial_query, state_transition, state_increment)

def causal_conv(values, kernel_vals):
    length_now = values.shape[0]
    padded = jnp.concatenate([jnp.zeros((KERNEL - 1, values.shape[1]), jnp.float32), values], axis=0)
    summed = kernel_vals[0] * padded[0:length_now]
    for offset in range(1, KERNEL):
        summed = summed + kernel_vals[offset] * padded[offset:offset + length_now]
    return summed

def stretch_step(carried_state, inputs):
    queries, key_rows, value_rows, beta_vals, log_decay = inputs
    shard_local_output, initial_query, state_transition, state_increment = stretch_parts(queries, key_rows, value_rows, beta_vals, log_decay)
    output_rows = shard_local_output + jnp.einsum('gtn,gnq->gtq', initial_query, carried_state, precision=FULL_PRODUCT)
    carried_state = jnp.einsum('zrm,zmd->zrd', state_transition, carried_state, precision=FULL_PRODUCT) + state_increment
    return (carried_state, output_rows)

def sequence_forward(weights, tokens, decays):
    mixer_gain, query_weight, key_weight, value_weight, beta_weight, outgate_weight, query_conv, key_conv, value_conv, head_gain, output_weight, feed_gain, feed_gate, feed_up, feed_down = weights
    length_now = tokens.shape[0]
    blocks = length_now // STRETCH
    normed = low(rms_scale(tokens, mixer_gain))
    query_pre = low(low_back(matmul(normed, query_weight)))
    key_pre = low(low_back(matmul(normed, key_weight)))
    value_pre = low(low_back(matmul(normed, value_weight)))
    gate_pre = low_back(matmul(normed, outgate_weight))
    beta_pre = low_back(matmul(normed, beta_weight))
    queries = low(unit_rows(jax.nn.silu(causal_conv(query_pre, query_conv)).reshape(length_now, H, DK)))
    key_rows = low(unit_rows(jax.nn.silu(causal_conv(key_pre, key_conv)).reshape(length_now, H, DK)))
    value_rows = low(jax.nn.silu(causal_conv(value_pre, value_conv)).reshape(length_now, H, DV))
    beta_vals = jax.nn.sigmoid(beta_pre)
    log_decay = jnp.log(decays)
    query_blocks = queries.reshape(blocks, STRETCH, H, DK).transpose(0, 2, 1, 3)
    key_blocks = key_rows.reshape(blocks, STRETCH, H, DK).transpose(0, 2, 1, 3)
    content_segments = value_rows.reshape(blocks, STRETCH, H, DV).transpose(0, 2, 1, 3)
    beta_blocks = beta_vals.reshape(blocks, STRETCH, H).transpose(0, 2, 1)
    decay_blocks = log_decay.reshape(H, blocks, STRETCH).transpose(1, 0, 2)
    starting_memory_matrix = jnp.zeros((H, DK, DV), jnp.float32)
    ending, head_blocks = lax.scan(jax.checkpoint(stretch_step), starting_memory_matrix, (query_blocks, key_blocks, content_segments, beta_blocks, decay_blocks))
    head_outputs = head_blocks.transpose(0, 2, 1, 3).reshape(length_now, H, DV)
    gated = rms_scale(head_outputs, head_gain) * jax.nn.silu(gate_pre).reshape(length_now, H, DV)
    mixed = low(gated.reshape(length_now, H * DV))
    middle = tokens + low_back(matmul(mixed, output_weight))
    feed_in = low(rms_scale(middle, feed_gain))
    gate_vals = low_back(matmul(feed_in, feed_gate))
    up_vals = low_back(matmul(feed_in, feed_up))
    hidden = low(jax.nn.silu(gate_vals) * up_vals)
    return middle + low_back(matmul(hidden, feed_down))

def reference(tokens, decays, out_grad, mixer_gain, query_weight, key_weight, value_weight, beta_weight, outgate_weight, query_conv, key_conv, value_conv, head_gain, output_weight, feed_gain, feed_gate, feed_up, feed_down):
    weights = tuple((member.astype(jnp.float32) for member in (mixer_gain, query_weight, key_weight, value_weight, beta_weight, outgate_weight, query_conv, key_conv, value_conv, head_gain, output_weight, feed_gain, feed_gate, feed_up, feed_down)))

    def one_sequence(sums, inputs):
        seq_tokens, seq_decays, seq_grad = inputs
        result, pullback = jax.vjp(lambda params, rows: sequence_forward(params, rows, seq_decays), weights, seq_tokens.astype(jnp.float32))
        weight_grads, token_grad = pullback(seq_grad.astype(jnp.float32))
        sums = jax.tree.map(lambda first, second: first + second, sums, weight_grads)
        return (sums, (result.astype(jnp.bfloat16), token_grad.astype(jnp.bfloat16)))
    zero_sums = jax.tree.map(jnp.zeros_like, weights)
    final, (output_rows, grads) = lax.scan(one_sequence, zero_sums, (tokens, decays, out_grad))
    return (output_rows, grads, final[0], final[1], final[2], final[3], final[4], final[5], final[6], final[7], final[8], final[9], final[10], final[11], final[12], final[13], final[14])
```

```python
import functools

import jax
import jax.numpy as jnp
from jax import lax
from jax.experimental import pallas as pl
from jax.experimental.pallas import tpu as pltpu
from jax.sharding import PartitionSpec as P

H = 16
DK = 128
DV = 256
CHUNK = 128
KERNEL = 4
HALO = 16
EPS_NORM = 1e-05
EPS_UNIT = 1e-06
F32 = jnp.float32
BF16 = jnp.bfloat16


def mm(a, b):
    return jnp.dot(a.astype(BF16), b.astype(BF16), preferred_element_type=F32)


def mm_nt(a, b):
    return lax.dot_general(
        a.astype(BF16), b.astype(BF16), (((1,), (1,)), ((), ())), preferred_element_type=F32
    )


def mm_tn(a, b):
    return lax.dot_general(
        a.astype(BF16), b.astype(BF16), (((0,), (0,)), ((), ())), preferred_element_type=F32
    )


def split_pair(a):
    high = a.astype(BF16)
    return high, (a - high.astype(F32)).astype(BF16)


def mm_fine(a, b):
    a_high, a_low = split_pair(a)
    b_high, b_low = split_pair(b)
    return (
        jnp.dot(a_high, b_high, preferred_element_type=F32)
        + jnp.dot(a_high, b_low, preferred_element_type=F32)
        + jnp.dot(a_low, b_high, preferred_element_type=F32)
    )


def sigmoid(v):
    return 1.0 / (1.0 + jnp.exp(-v))


def conv_cols(ext, seq, start, width, taps, rows):
    total = None
    for tap in range(KERNEL):
        term = taps[tap : tap + 1, start : start + width] * ext[
            seq, pl.ds(8 - (KERNEL - 1) + tap, rows), start : start + width
        ]
        total = term if total is None else total + term
    return total


def lower_masks(rows):
    row = lax.broadcasted_iota(jnp.int32, (rows, rows), 0)
    col = lax.broadcasted_iota(jnp.int32, (rows, rows), 1)
    return row, col


def inverse_many(couplings, row, col):
    rows = row.shape[0]
    eye = (row == col).astype(F32)
    pair = (row // 2 == col // 2)
    out = [eye - jnp.where(pair, a, 0.0) for a in couplings]
    size = 2
    while size < rows:
        mask = (row // (2 * size) == col // (2 * size)) & (row // size != col // size)
        inner = [mm_fine(jnp.where(mask, a, 0.0), t) for a, t in zip(couplings, out)]
        out = [t - mm_fine(t, i) for t, i in zip(out, inner)]
        size *= 2
    return out


def forward_body(
    heads, place, pre, gate, cols, rows_g, taps, gain, mixed, outs, fresh, starts, solved, ext, state
):
    chunk = pl.program_id(0)
    count = pre.shape[1]
    key_all = heads * DK

    @pl.when(chunk == 0)
    def _():
        ext[:, 0:8, :] = jnp.zeros((2, 8, ext.shape[2]), F32)
        state[...] = jnp.zeros(state.shape, F32)

    row, col = lower_masks(count)
    streams = [(seq, head) for seq in range(2) for head in range(heads)]
    for seq in range(2):
        ext[seq, 8 : 8 + count, :] = pre[seq].astype(F32)
    queries, keys, values, ratios, couplings = [], [], [], [], []
    for seq, head in streams:
        q = conv_cols(ext, seq, head * DK, DK, taps, count)
        q = q * sigmoid(q)
        q = q * lax.rsqrt(jnp.sum(q * q, axis=1, keepdims=True) + EPS_UNIT)
        k = conv_cols(ext, seq, key_all + head * DK, DK, taps, count)
        k = k * sigmoid(k)
        k = k * lax.rsqrt(jnp.sum(k * k, axis=1, keepdims=True) + EPS_UNIT)
        v = conv_cols(ext, seq, 2 * key_all + head * DV, DV, taps, count)
        v = v * sigmoid(v)
        queries.append(q.astype(BF16))
        keys.append(k.astype(BF16))
        values.append(v.astype(BF16))
        g_col = cols[seq, :, 4 * head + 1 : 4 * head + 2]
        g_row = rows_g[seq, 0, head : head + 1, :]
        ratio = jnp.where(row >= col, jnp.exp(jnp.minimum(g_col - g_row, 0.0)), 0.0)
        ratios.append(ratio)
        beta = cols[seq, :, 4 * head : 4 * head + 1]
        couplings.append(jnp.where(row > col, beta * ratio * mm_nt(keys[-1], keys[-1]), 0.0))
    for seq in range(2):
        ext[seq, 0:8, :] = ext[seq, count : count + 8, :]
    inverses = inverse_many(couplings, row, col)
    for at, (seq, head) in enumerate(streams):
        q, k, v, ratio = queries[at], keys[at], values[at], ratios[at]
        beta = cols[seq, :, 4 * head : 4 * head + 1]
        grown = cols[seq, :, 4 * head + 2 : 4 * head + 3]
        fade = cols[seq, :, 4 * head + 3 : 4 * head + 4]
        held = state[at]
        held_low = held.astype(BF16)
        starts[0, at] = held_low
        inverse = inverses[at].astype(BF16)
        solved[0, at] = inverse
        right = beta * (v.astype(F32) - grown * mm(k, held_low))
        news = mm(inverse, right).astype(BF16)
        scores = ratio * mm_nt(q, k)
        out = mm(scores, news) + grown * mm(q, held_low)
        last = jnp.exp(rows_g[seq, 0, head : head + 1, count - 1 : count])
        state[at] = last * held + mm_tn(fade * k.astype(F32), news)
        place_v = slice(head * DV, head * DV + DV)
        fresh[seq, :, place_v] = news
        outs[seq, :, place_v] = out.astype(BF16)
        scale = lax.rsqrt(jnp.mean(out * out, axis=1, keepdims=True) + EPS_NORM)
        g = gate[seq, :, place_v].astype(F32)
        mixed[seq, :, place_v] = (out * scale * gain[0:1, :] * (g * sigmoid(g))).astype(BF16)


def backward_body(
    heads,
    place,
    pre,
    halo,
    d_outs,
    cols,
    rows_g,
    taps,
    fresh,
    starts,
    solved,
    d_pre,
    d_beta,
    d_taps,
    ext,
    d_ext,
    d_state,
):
    step = pl.program_id(0)
    chunk = pl.num_programs(0) - 1 - step
    count = pre.shape[1]
    key_all = heads * DK

    @pl.when(step == 0)
    def _():
        d_ext[:, count : count + 8, :] = jnp.zeros((2, 8, d_ext.shape[2]), F32)
        d_state[...] = jnp.zeros(d_state.shape, F32)
        d_taps[...] = jnp.zeros(d_taps.shape, F32)

    row, col = lower_masks(count)
    streams = [(seq, head) for seq in range(2) for head in range(heads)]
    keep = jnp.where(chunk > 0, 1.0, 0.0)
    for seq in range(2):
        ext[seq, 0:8, :] = keep * halo[seq].astype(F32)[HALO - 8 : HALO, :]
        ext[seq, 8 : 8 + count, :] = pre[seq].astype(F32)
    d_betas = []
    for at, (seq, head) in enumerate(streams):
        beta = cols[seq, :, 4 * head : 4 * head + 1]
        g_col = cols[seq, :, 4 * head + 1 : 4 * head + 2]
        grown = cols[seq, :, 4 * head + 2 : 4 * head + 3]
        fade = cols[seq, :, 4 * head + 3 : 4 * head + 4]
        g_row = rows_g[seq, 0, head : head + 1, :]
        last = jnp.exp(g_row[:, count - 1 : count])

        q_conv = conv_cols(ext, seq, head * DK, DK, taps, count)
        q_sig = sigmoid(q_conv)
        q_act = q_conv * q_sig
        q_scale = lax.rsqrt(jnp.sum(q_act * q_act, axis=1, keepdims=True) + EPS_UNIT)
        q_unit = q_act * q_scale
        k_conv = conv_cols(ext, seq, key_all + head * DK, DK, taps, count)
        k_sig = sigmoid(k_conv)
        k_act = k_conv * k_sig
        k_scale = lax.rsqrt(jnp.sum(k_act * k_act, axis=1, keepdims=True) + EPS_UNIT)
        k_unit = k_act * k_scale
        v_conv = conv_cols(ext, seq, 2 * key_all + head * DV, DV, taps, count)
        v_sig = sigmoid(v_conv)
        q, k = q_unit.astype(BF16), k_unit.astype(BF16)
        v = (v_conv * v_sig).astype(BF16).astype(F32)
        k_full = k.astype(F32)

        place_v = slice(head * DV, head * DV + DV)
        d_out = d_outs[seq, :, place_v]
        news = fresh[seq, :, place_v]
        held = starts[0, at]
        inverse = solved[0, at]
        d_held = d_state[at]
        d_held_low = d_held.astype(BF16)
        ratio = jnp.where(row >= col, jnp.exp(jnp.minimum(g_col - g_row, 0.0)), 0.0)
        scores = ratio * mm_nt(q, k)
        d_news = mm_tn(scores, d_out) + mm(fade * k_full, d_held_low)
        d_right = mm_tn(inverse, d_news)
        d_right_low = d_right.astype(BF16)
        d_couple = jnp.where(row > col, -ratio * mm_nt(d_right_low, news), 0.0)
        key_key = mm_nt(k, k)
        d_kk = beta * d_couple
        d_scores = ratio * mm_nt(d_out, news)
        out_held = mm_nt(d_out, held)
        right_held = mm_nt(d_right_low, held)
        news_held = mm_nt(news, d_held_low)
        d_q = mm(d_scores, k) + grown * out_held
        d_k = (
            mm_tn(d_scores, q)
            + mm(d_kk, k)
            + mm_tn(d_kk, k)
            + fade * news_held
            - (beta * grown) * right_held
        )
        d_v = beta * d_right
        d_betas.append(
            jnp.sum(d_right * v, axis=1, keepdims=True)
            - grown * jnp.sum(right_held * k_full, axis=1, keepdims=True)
            + jnp.sum(d_couple * key_key, axis=1, keepdims=True)
        )
        d_state[at] = (
            last * d_held
            + mm_tn(grown * q.astype(F32), d_out)
            - mm_tn((beta * grown) * k_full, d_right_low)
        )
        d_qa = q_scale * (d_q - q_unit * jnp.sum(q_unit * d_q, axis=1, keepdims=True))
        d_ka = k_scale * (d_k - k_unit * jnp.sum(k_unit * d_k, axis=1, keepdims=True))
        d_ext[seq, 0:count, head * DK : head * DK + DK] = d_qa * (
            q_sig * (1.0 + q_conv * (1.0 - q_sig))
        )
        d_ext[seq, 0:count, key_all + head * DK : key_all + head * DK + DK] = d_ka * (
            k_sig * (1.0 + k_conv * (1.0 - k_sig))
        )
        d_ext[
            seq, 0:count, 2 * key_all + head * DV : 2 * key_all + head * DV + DV
        ] = d_v * (v_sig * (1.0 + v_conv * (1.0 - v_sig)))
    for seq in range(2):
        for head in range(heads):
            beta = cols[seq, :, 4 * head : 4 * head + 1]
            d_beta[seq, :, head : head + 1] = d_betas[seq * heads + head] * beta * (1.0 - beta)
        wide = ext.shape[2]
        for start in range(0, wide, 128):
            span = slice(start, start + 128)
            total = None
            near = d_ext[seq, 0:count, span]
            for tap in range(KERNEL):
                term = taps[tap : tap + 1, span] * d_ext[seq, pl.ds(KERNEL - 1 - tap, count), span]
                total = term if total is None else total + term
                moved = ext[seq, pl.ds(8 - (KERNEL - 1) + tap, count), span]
                d_taps[tap : tap + 1, span] += jnp.sum(near * moved, axis=0, keepdims=True)
            d_pre[seq, :, span] = total.astype(BF16)
        d_ext[seq, count : count + 8, :] = d_ext[seq, 0:8, :]


def gating_body(heads, d_mixed_a, d_mixed_b, outs, gate, gain, d_outs, d_gate, d_gain):
    @pl.when(pl.program_id(0) == 0)
    def _():
        d_gain[...] = jnp.zeros(d_gain.shape, F32)

    total = None
    for seq, d_mixed in ((0, d_mixed_a), (1, d_mixed_b)):
        for head in range(heads):
            span = slice(head * DV, head * DV + DV)
            out = outs[seq, :, span].astype(F32)
            grad = d_mixed[:, span].astype(F32)
            g = gate[seq, :, span].astype(F32)
            sig = sigmoid(g)
            scale = lax.rsqrt(jnp.mean(out * out, axis=1, keepdims=True) + EPS_NORM)
            unit = out * scale
            cot = grad * (g * sig)
            term = jnp.sum(cot * unit, axis=0, keepdims=True)
            total = term if total is None else total + term
            scaled = cot * gain[0:1, :]
            d_outs[seq, :, span] = (
                scale * (scaled - unit * jnp.mean(unit * scaled, axis=1, keepdims=True))
            ).astype(BF16)
            d_gate[seq, :, span] = (
                grad * unit * gain[0:1, :] * (sig * (1.0 + g * (1.0 - sig)))
            ).astype(BF16)
    d_gain[0:1, :] += total


def chunk_place(chunk, place, per_piece):
    piece = chunk // per_piece
    return jnp.bitwise_xor(piece, place[0]) * per_piece + chunk % per_piece


def run_forward(place, piece_rows, pre, gate, cols, rows_g, taps, gain):
    _, length, wide = pre.shape
    heads = gate.shape[2] // DV
    chunks = length // CHUNK
    per_piece = piece_rows // CHUNK

    def by_rows(width):
        return pl.BlockSpec(
            (2, CHUNK, width), lambda c, at: (0, chunk_place(c, at, per_piece), 0)
        )

    grid_spec = pltpu.PrefetchScalarGridSpec(
        num_scalar_prefetch=1,
        grid=(chunks,),
        in_specs=[
            by_rows(wide),
            by_rows(heads * DV),
            by_rows(4 * heads),
            pl.BlockSpec(
                (2, 1, heads, CHUNK), lambda c, at: (0, chunk_place(c, at, per_piece), 0, 0)
            ),
            pl.BlockSpec((8, wide), lambda c, at: (0, 0)),
            pl.BlockSpec((1, DV), lambda c, at: (0, 0)),
        ],
        out_specs=[
            by_rows(heads * DV),
            by_rows(heads * DV),
            by_rows(heads * DV),
            pl.BlockSpec((1, 2 * heads, DK, DV), lambda c, at: (c, 0, 0, 0)),
            pl.BlockSpec((1, 2 * heads, CHUNK, CHUNK), lambda c, at: (c, 0, 0, 0)),
        ],
        scratch_shapes=[
            pltpu.VMEM((2, CHUNK + 8, wide), F32),
            pltpu.VMEM((2 * heads, DK, DV), F32),
        ],
    )
    rows_out = jax.ShapeDtypeStruct((2, length, heads * DV), BF16)
    return pl.pallas_call(
        functools.partial(forward_body, heads),
        grid_spec=grid_spec,
        out_shape=[
            rows_out,
            rows_out,
            rows_out,
            jax.ShapeDtypeStruct((chunks, 2 * heads, DK, DV), BF16),
            jax.ShapeDtypeStruct((chunks, 2 * heads, CHUNK, CHUNK), BF16),
        ],
        compiler_params=pltpu.CompilerParams(
            dimension_semantics=("arbitrary",), vmem_limit_bytes=40 * 1024 * 1024
        ),
        name="delta_forward",
    )(place, pre, gate, cols, rows_g, taps, gain)


def run_backward(place, piece_rows, pre, d_outs, cols, rows_g, taps, fresh, starts, solved):
    _, length, wide = pre.shape
    heads = d_outs.shape[2] // DV
    chunks = length // CHUNK
    per_piece = piece_rows // CHUNK
    per_halo = CHUNK // HALO

    def turned(step):
        return chunks - 1 - step

    def by_rows(width):
        return pl.BlockSpec(
            (2, CHUNK, width), lambda c, at: (0, chunk_place(turned(c), at, per_piece), 0)
        )

    def halo_place(step, at):
        before = jnp.maximum(turned(step) - 1, 0)
        return (0, chunk_place(before, at, per_piece) * per_halo + per_halo - 1, 0)

    grid_spec = pltpu.PrefetchScalarGridSpec(
        num_scalar_prefetch=1,
        grid=(chunks,),
        in_specs=[
            by_rows(wide),
            pl.BlockSpec((2, HALO, wide), halo_place),
            by_rows(heads * DV),
            by_rows(4 * heads),
            pl.BlockSpec(
                (2, 1, heads, CHUNK),
                lambda c, at: (0, chunk_place(turned(c), at, per_piece), 0, 0),
            ),
            pl.BlockSpec((8, wide), lambda c, at: (0, 0)),
            by_rows(heads * DV),
            pl.BlockSpec((1, 2 * heads, DK, DV), lambda c, at: (turned(c), 0, 0, 0)),
            pl.BlockSpec((1, 2 * heads, CHUNK, CHUNK), lambda c, at: (turned(c), 0, 0, 0)),
        ],
        out_specs=[
            by_rows(wide),
            by_rows(heads),
            pl.BlockSpec((8, wide), lambda c, at: (0, 0)),
        ],
        scratch_shapes=[
            pltpu.VMEM((2, CHUNK + 8, wide), F32),
            pltpu.VMEM((2, CHUNK + 8, wide), F32),
            pltpu.VMEM((2 * heads, DK, DV), F32),
        ],
    )
    return pl.pallas_call(
        functools.partial(backward_body, heads),
        grid_spec=grid_spec,
        out_shape=[
            jax.ShapeDtypeStruct((2, length, wide), BF16),
            jax.ShapeDtypeStruct((2, length, heads), F32),
            jax.ShapeDtypeStruct((8, wide), F32),
        ],
        compiler_params=pltpu.CompilerParams(
            dimension_semantics=("arbitrary",), vmem_limit_bytes=40 * 1024 * 1024
        ),
        name="delta_backward",
    )(place, pre, pre, d_outs, cols, rows_g, taps, fresh, starts, solved)


def run_gating(d_mixed_a, d_mixed_b, outs, gate, gain):
    _, length, wide = outs.shape
    heads = wide // DV
    tile = 256
    both = pl.BlockSpec((2, tile, wide), lambda c: (0, c, 0))
    one = pl.BlockSpec((tile, wide), lambda c: (c, 0))
    shape = jax.ShapeDtypeStruct((2, length, wide), BF16)
    return pl.pallas_call(
        functools.partial(gating_body, heads),
        grid=(length // tile,),
        in_specs=[one, one, both, both, pl.BlockSpec((1, DV), lambda c: (0, 0))],
        out_specs=[both, both, pl.BlockSpec((8, DV), lambda c: (0, 0))],
        out_shape=[shape, shape, jax.ShapeDtypeStruct((8, DV), F32)],
        compiler_params=pltpu.CompilerParams(
            dimension_semantics=("arbitrary",), vmem_limit_bytes=40 * 1024 * 1024
        ),
        name="gating_backward",
    )(d_mixed_a, d_mixed_b, outs, gate, gain)


def product(left_side, right_side):
    return jnp.dot(left_side, right_side, preferred_element_type=F32)


def product_tn(left_side, right_side):
    return lax.dot_general(
        left_side, right_side, (((0,), (0,)), ((), ())), preferred_element_type=F32
    )


def product_nt(left_side, right_side):
    return lax.dot_general(
        left_side, right_side, (((1,), (1,)), ((), ())), preferred_element_type=F32
    )


def rms_scale(values, gain_vals):
    return (
        values * lax.rsqrt(jnp.mean(values * values, axis=-1, keepdims=True) + EPS_NORM) * gain_vals
    )


def swap(values, axis, bit):
    count = lax.axis_size(axis)
    return lax.ppermute(values, axis, [(place, place ^ bit) for place in range(count)])


def bits_of(count):
    found = []
    bit = 1
    while bit < count:
        found.append(bit)
        bit *= 2
    return found


def after(values, *earlier):
    return lax.optimization_barrier((values, *earlier))[0]


def add_low(left_side, right_side):
    return (left_side.astype(F32) + right_side.astype(F32)).astype(BF16)


def spread_rows(own, team):
    seq_count = lax.axis_size("seq")

    def along_seq(first):
        pieces = {0: first}
        for offset in sorted(range(1, seq_count), key=lambda o: -(o & -o)):
            low = offset & -offset
            pieces[offset] = swap(pieces[offset ^ low], "seq", low)
        return [pieces[offset] for offset in range(seq_count)]

    other = swap(own, "batch", team)
    return along_seq(own), along_seq(other)


def sum_rows(part_own, part_other, team):
    seq_count = lax.axis_size("seq")
    rows = part_own.shape[0] // seq_count

    def along_seq(part):
        pieces = {at: part[at * rows : (at + 1) * rows] for at in range(seq_count)}
        for bit in bits_of(seq_count):
            for at in [place for place in pieces if place & bit]:
                came = swap(pieces.pop(at), "seq", bit)
                pieces[at ^ bit] = add_low(pieces[at ^ bit], came)
        return pieces[0]

    came = swap(along_seq(part_other), "batch", team)
    return along_seq(part_own).astype(F32) + came.astype(F32)


def spread_all(values):
    values = values[None]
    for axis in ("batch", "seq"):
        place = lax.axis_index(axis)
        for bit in bits_of(lax.axis_size(axis)):
            came = swap(values, axis, bit)
            values = jnp.where(
                (place & bit) == 0,
                jnp.concatenate([values, came], axis=0),
                jnp.concatenate([came, values], axis=0),
            )
    return values


def sum_all(values):
    for axis in ("seq", "batch"):
        place = lax.axis_index(axis)
        for bit in reversed(bits_of(lax.axis_size(axis))):
            half = values.shape[0] // 2
            upper = (place & bit) != 0
            keep = jnp.where(upper, values[half:], values[:half])
            send = jnp.where(upper, values[:half], values[half:])
            values = keep + swap(send, axis, bit)
    return values[0]


def local(
    tokens,
    decays,
    out_grad,
    mixer_gain,
    query_weight,
    key_weight,
    value_weight,
    beta_weight,
    outgate_weight,
    query_conv,
    key_conv,
    value_conv,
    head_gain,
    output_weight,
    feed_gain,
    feed_gate,
    feed_up,
    feed_down,
):
    seq_count = lax.axis_size("seq")
    batch_count = lax.axis_size("batch")
    seq_pos = lax.axis_index("seq")
    batch_pos = lax.axis_index("batch")
    devices = seq_count * batch_count
    team = devices // H
    heads = H // (2 * seq_count)
    offsets = [offset for offset in range(batch_count) if not offset & team]
    source = tokens[0]
    grad_own = out_grad[0]
    rows, model = source.shape
    length = rows * seq_count
    key_part = query_weight.shape[1]
    value_part = value_weight.shape[1]
    feed_part = feed_gate.shape[1]
    gain_part = mixer_gain.shape[0]
    head_part = head_gain.shape[0]

    small = jnp.concatenate(
        [mixer_gain, feed_gain, beta_weight.T.reshape(-1), head_gain], axis=0
    )
    small_size = small.shape[0]
    small = jnp.pad(small, (0, -small_size % 2048)).reshape(-1, 128)
    small_all = spread_all(small).reshape(devices, -1)
    gain_f = small_all[:, :gain_part].reshape(-1).astype(F32)
    feed_gain_f = small_all[:, gain_part : 2 * gain_part].reshape(-1).astype(F32)
    beta_rows = (
        small_all[:, 2 * gain_part : 2 * gain_part + H * gain_part]
        .reshape(devices, H, gain_part)
        .transpose(1, 0, 2)
        .reshape(H, model)
    )
    head_gain_all = small_all[:, small_size - head_part : small_size].reshape(-1)
    inner = batch_pos % team
    gain_blocks = head_gain_all.reshape(team, DV // team)
    head_gain_f = jnp.concatenate(
        [lax.dynamic_index_in_dim(gain_blocks, at ^ inner, 0, False) for at in range(team)], axis=0
    ).astype(F32)
    head_places = [
        seq_pos * (H // seq_count) + ((batch_pos // team) ^ (2 * head)) for head in range(heads)
    ]
    beta_own = jnp.stack(
        [lax.dynamic_index_in_dim(beta_rows, place, 0, False) for place in head_places], axis=0
    )

    taps_own = jnp.concatenate([query_conv, key_conv, value_conv], axis=1)
    taps_wide = taps_own.shape[1]
    taps_rows = jnp.pad(taps_own.reshape(-1), (0, -taps_own.size % (16 * model))).reshape(-1, model)
    shares = [
        jnp.concatenate([query_weight.T, key_weight.T, value_weight.T, taps_rows], axis=0),
        jnp.concatenate([outgate_weight.T, output_weight], axis=0),
        jnp.concatenate([feed_gate.T, feed_up.T], axis=0),
        feed_down,
    ]
    spread = []
    far_chain, near_chain = [], []
    for share in shares:
        pieces = {0: share}
        for offset in sorted(offsets[1:], key=lambda o: (-(o & -o), o)):
            low = offset & -offset
            chain = far_chain if low > team else near_chain
            send = pieces[offset ^ low]
            if len(chain) >= 2:
                send = after(send, chain[-2])
            pieces[offset] = swap(send, "batch", low)
            chain.append(pieces[offset])
        spread.append([pieces[offset] for offset in offsets])

    def joined(pieces, start, size):
        return [piece[start : start + size] for piece in pieces]

    mix_rows = jnp.concatenate(
        joined(spread[0], 0, key_part)
        + joined(spread[0], key_part, key_part)
        + joined(spread[0], 2 * key_part, value_part),
        axis=0,
    )
    taps_at = 2 * key_part + value_part
    taps_all = [
        piece[taps_at:].reshape(-1)[: KERNEL * taps_wide].reshape(KERNEL, taps_wide)
        for piece in spread[0]
    ]
    taps = jnp.concatenate(
        [piece[:, :key_part] for piece in taps_all]
        + [piece[:, key_part : 2 * key_part] for piece in taps_all]
        + [piece[:, 2 * key_part :] for piece in taps_all],
        axis=1,
    ).astype(F32)
    taps = jnp.pad(taps, ((0, 8 - KERNEL), (0, 0)))
    gate_rows = jnp.concatenate(joined(spread[1], 0, value_part), axis=0)
    out_rows = jnp.concatenate(joined(spread[1], value_part, value_part), axis=0)
    feed_rows = jnp.concatenate(
        joined(spread[2], 0, feed_part) + joined(spread[2], feed_part, feed_part), axis=0
    )
    down_rows = jnp.concatenate(spread[3], axis=0)
    feed_here = down_rows.shape[0]

    own_rows, other_rows = spread_rows(source, team)
    both_tokens = jnp.concatenate(own_rows + other_rows, axis=0)
    both_f = both_tokens.astype(F32)
    unit_f = both_f * lax.rsqrt(jnp.mean(both_f * both_f, axis=-1, keepdims=True) + EPS_NORM)
    normed = (unit_f * gain_f).astype(BF16)
    own_grads, other_grads = spread_rows(after(grad_own, other_rows[-1]), team)
    seq_grads = [jnp.concatenate(own_grads, axis=0), jnp.concatenate(other_grads, axis=0)]

    logs = jnp.log(decays[0])[None]
    logs = jnp.concatenate([logs, swap(logs, "batch", team)], axis=0)[:, None]
    for bit in bits_of(seq_count):
        logs = jnp.concatenate([logs, swap(logs, "seq", bit)], axis=1)
    head_logs = jnp.stack(
        [lax.dynamic_index_in_dim(logs, place, 2, False) for place in head_places], axis=1
    )
    chunks = length // CHUNK
    totals = jnp.cumsum(head_logs.reshape(2, heads, chunks, CHUNK), axis=-1)
    rows_g = totals.transpose(0, 2, 1, 3)
    totals_cols = totals.reshape(2, heads, length).transpose(0, 2, 1)
    fade_cols = (
        jnp.exp(totals[..., -1:] - totals).reshape(2, heads, length).transpose(0, 2, 1)
    )

    pre = product_nt(normed, mix_rows).astype(BF16).reshape(2, length, -1)
    beta_pre = product_nt(normed, beta_own).reshape(2, length, heads)
    gate_pre = product_nt(normed, gate_rows).astype(BF16).reshape(2, length, -1)
    cols = jnp.stack(
        [jax.nn.sigmoid(beta_pre), totals_cols, jnp.exp(totals_cols), fade_cols], axis=-1
    ).reshape(2, length, 4 * heads)
    place = jnp.full((1,), seq_pos, jnp.int32)
    gain_row = head_gain_f[None]
    mixed, head_outs, fresh, starts, solved = run_forward(
        place, rows, pre, gate_pre, cols, rows_g, taps, gain_row
    )
    branch = [product(mixed[at], out_rows).astype(BF16) for at in range(2)]
    source_f = source.astype(F32)
    middle = source_f + sum_rows(branch[0], branch[1], team)

    feed_in = rms_scale(middle, feed_gain_f).astype(BF16)
    own_feed, other_feed = spread_rows(feed_in, team)
    seq_feed = [jnp.concatenate(own_feed, axis=0), jnp.concatenate(other_feed, axis=0)]
    down_parts, feed_backs = [], []
    down_term, feed_term = 0.0, 0.0
    for feed, grad in zip(seq_feed, seq_grads):
        gate_vals = product_nt(feed_rows[:feed_here], feed)
        up_vals = product_nt(feed_rows[feed_here:], feed)
        gate_sig = jax.nn.sigmoid(gate_vals)
        hidden = (gate_vals * gate_sig * up_vals).astype(BF16)
        d_hidden = product_nt(down_rows, grad)
        d_gate = d_hidden * up_vals * gate_sig * (1.0 + gate_vals * (1.0 - gate_sig))
        d_up = d_hidden * gate_vals * gate_sig
        d_both = jnp.concatenate([d_gate.astype(BF16), d_up.astype(BF16)], axis=0)
        feed_backs.append(product_tn(d_both, feed_rows).astype(BF16))
        down_parts.append(product_tn(hidden, down_rows).astype(BF16))
        down_term = down_term + product(hidden, grad)
        feed_term = feed_term + product(d_both, feed)
    d_feed_in = sum_rows(feed_backs[0], feed_backs[1], team)
    feed_pull = jax.vjp(rms_scale, middle, feed_gain_f)[1]
    d_mid_norm, feed_gain_term = feed_pull(d_feed_in)
    d_middle = grad_own.astype(F32) + d_mid_norm
    d_branch = d_middle.astype(BF16)
    own_branch, other_branch = spread_rows(d_branch, team)
    both_branch = jnp.concatenate(own_branch + other_branch, axis=0)
    down_ready = [after(part, other_branch[-1]) for part in down_parts]
    block_out = (middle + sum_rows(down_ready[0], down_ready[1], team)).astype(BF16)[None]

    d_mixed = product_nt(both_branch, out_rows).astype(BF16)
    d_outs, d_gate_pre, head_gain_term = run_gating(
        d_mixed[:length], d_mixed[length:], head_outs, gate_pre, gain_row
    )
    d_pre, d_beta, d_taps = run_backward(
        place, rows, pre, d_outs, cols, rows_g, taps, fresh, starts, solved
    )
    d_beta_low = d_beta.astype(BF16)
    d_normed = [
        product(d_pre[at], mix_rows)
        + product(d_gate_pre[at], gate_rows)
        + product(d_beta_low[at], beta_own)
        for at in range(2)
    ]
    d_normed_low = [part.astype(BF16) for part in d_normed]

    output_term = product_tn(mixed.reshape(2 * length, -1), both_branch).astype(BF16)
    outgate_term = product_tn(d_gate_pre.reshape(2 * length, -1), normed).astype(BF16)
    mix_term = product_tn(d_pre.reshape(2 * length, -1), normed).astype(BF16)
    beta_term = product_tn(d_beta_low.reshape(2 * length, -1), normed)
    mixer_gain_term = sum(
        jnp.sum(d_normed[at] * unit_f[at * length : (at + 1) * length], axis=0) for at in range(2)
    )

    def collect(pieces):
        pieces = dict(zip(offsets, pieces))
        for bit in bits_of(batch_count):
            if bit == team:
                continue
            for offset in sorted((o for o in pieces if o & bit), reverse=True):
                came = swap(pieces.pop(offset), "batch", bit)
                left = pieces[offset ^ bit].astype(F32) + came.astype(F32)
                pieces[offset ^ bit] = left if offset == bit and len(pieces) == 1 else left.astype(BF16)
        return pieces[0]

    def cut(values, at, size):
        return values[at * size : (at + 1) * size]

    count = len(offsets)
    down_low = down_term.astype(BF16)
    feed_low = feed_term.astype(BF16)
    down_sum = collect([cut(down_low, at, feed_part) for at in range(count)])
    feed_sum = collect(
        [
            jnp.concatenate(
                [cut(feed_low[:feed_here], at, feed_part), cut(feed_low[feed_here:], at, feed_part)],
                axis=0,
            )
            for at in range(count)
        ]
    )
    gate_sum = collect(
        [
            jnp.concatenate(
                [cut(outgate_term, at, value_part), cut(output_term, at, value_part)], axis=0
            )
            for at in range(count)
        ]
    )
    key_here = count * key_part
    taps_low = d_taps[:KERNEL].astype(BF16)

    def taps_piece(at):
        flat = jnp.concatenate(
            [
                taps_low[:, at * key_part : (at + 1) * key_part],
                taps_low[:, key_here + at * key_part : key_here + (at + 1) * key_part],
                taps_low[:, 2 * key_here + at * value_part : 2 * key_here + (at + 1) * value_part],
            ],
            axis=1,
        ).reshape(-1)
        return jnp.pad(flat, (0, -flat.size % (16 * model))).reshape(-1, model)

    mix_sum = collect(
        [
            jnp.concatenate(
                [
                    cut(mix_term[:key_here], at, key_part),
                    cut(mix_term[key_here : 2 * key_here], at, key_part),
                    cut(mix_term[2 * key_here :], at, value_part),
                    taps_piece(at),
                ],
                axis=0,
            )
            for at in range(count)
        ]
    )
    taps_sum = mix_sum[taps_at:].reshape(-1)[: KERNEL * taps_wide].reshape(KERNEL, taps_wide)

    head_terms = head_gain_term[0].reshape(team, DV // team)
    head_terms = jnp.concatenate(
        [lax.dynamic_index_in_dim(head_terms, at ^ inner, 0, False) for at in range(team)], axis=0
    )
    beta_all = jnp.zeros((H, model), F32)
    for head in range(heads):
        beta_all = lax.dynamic_update_slice(
            beta_all, beta_term[head : head + 1], (head_places[head], jnp.int32(0))
        )
    small_terms = jnp.concatenate(
        [
            mixer_gain_term.reshape(devices, gain_part),
            feed_gain_term.reshape(devices, gain_part),
            beta_all.reshape(H, devices, gain_part).transpose(1, 0, 2).reshape(devices, -1),
            head_terms.reshape(devices, head_part),
        ],
        axis=1,
    )
    small_terms = jnp.pad(small_terms, ((0, 0), (0, -small_size % 1024)))
    small_sum = sum_all(small_terms.reshape(devices, -1, 128)).reshape(-1)
    beta_sum = small_sum[2 * gain_part : 2 * gain_part + H * gain_part].reshape(H, gain_part).T

    d_source = sum_rows(d_normed_low[0], d_normed_low[1], team)
    mixer_pull = jax.vjp(lambda vals: rms_scale(vals, gain_f), source_f)[1]
    tokens_grad = (d_middle + mixer_pull(d_source)[0]).astype(BF16)[None]

    return (
        block_out,
        tokens_grad,
        small_sum[:gain_part],
        mix_sum[:key_part].T,
        mix_sum[key_part : 2 * key_part].T,
        mix_sum[2 * key_part : taps_at].T,
        beta_sum,
        gate_sum[:value_part].T,
        taps_sum[:, :key_part],
        taps_sum[:, key_part : 2 * key_part],
        taps_sum[:, 2 * key_part :],
        small_sum[small_size - head_part : small_size],
        gate_sum[value_part:],
        small_sum[gain_part : 2 * gain_part],
        feed_sum[:feed_part].T,
        feed_sum[feed_part:].T,
        down_sum,
    )


def solution(mesh):
    in_specs = (
        P("batch", "seq", None),
        P("batch", None, "seq"),
        P("batch", "seq", None),
        P(("seq", "batch")),
        P(None, ("seq", "batch")),
        P(None, ("seq", "batch")),
        P(None, ("seq", "batch")),
        P(("seq", "batch"), None),
        P(None, ("seq", "batch")),
        P(None, ("seq", "batch")),
        P(None, ("seq", "batch")),
        P(None, ("seq", "batch")),
        P(("seq", "batch")),
        P(("seq", "batch"), None),
        P(("seq", "batch")),
        P(None, ("seq", "batch")),
        P(None, ("seq", "batch")),
        P(("seq", "batch"), None),
    )
    out_specs = (
        P("batch", "seq", None),
        P("batch", "seq", None),
        P(("seq", "batch")),
        P(None, ("seq", "batch")),
        P(None, ("seq", "batch")),
        P(None, ("seq", "batch")),
        P(("seq", "batch"), None),
        P(None, ("seq", "batch")),
        P(None, ("seq", "batch")),
        P(None, ("seq", "batch")),
        P(None, ("seq", "batch")),
        P(("seq", "batch")),
        P(("seq", "batch"), None),
        P(("seq", "batch")),
        P(None, ("seq", "batch")),
        P(None, ("seq", "batch")),
        P(("seq", "batch"), None),
    )
    return jax.shard_map(local, mesh=mesh, in_specs=in_specs, out_specs=out_specs, check_vma=False)
```

```python
import functools

import jax
import jax.numpy as jnp
from jax import lax
from jax.experimental import pallas as pl
from jax.experimental.pallas import tpu as pltpu
from jax.sharding import Mesh, PartitionSpec as P

H = 16
DK = 128
DV = 256
CHUNK = 128
KERNEL = 4
HALO = 16
BETA_LANES = 128
BATCH = ("high", "team", "low")
ALL = ("seq", "high", "team", "low")
EPS_NORM = 1e-05
EPS_UNIT = 1e-06
F32 = jnp.float32
BF16 = jnp.bfloat16
VMEM_PARAMS = pltpu.CompilerParams(
    dimension_semantics=("arbitrary",), vmem_limit_bytes=52 * 1024 * 1024
)


def mm(a, b):
    return jnp.dot(a.astype(BF16), b.astype(BF16), preferred_element_type=F32)


def mm_nt(a, b):
    return lax.dot_general(
        a.astype(BF16), b.astype(BF16), (((1,), (1,)), ((), ())), preferred_element_type=F32
    )


def mm_tn(a, b):
    return lax.dot_general(
        a.astype(BF16), b.astype(BF16), (((0,), (0,)), ((), ())), preferred_element_type=F32
    )


def split_pair(a):
    high = a.astype(BF16)
    return high, (a - high.astype(F32)).astype(BF16)


def mm_fine(a, b):
    a_high, a_low = split_pair(a)
    b_high, b_low = split_pair(b)
    left = jnp.concatenate([a_high, a_low], axis=1)
    right = jnp.concatenate(
        [
            jnp.concatenate([b_high, b_low], axis=1),
            jnp.concatenate([b_high, jnp.zeros_like(b_low)], axis=1),
        ],
        axis=0,
    )
    both = jnp.dot(left, right, preferred_element_type=F32)
    wide = b.shape[1]
    return both[:, :wide] + both[:, wide:]


def sigmoid(v):
    return 1.0 / (1.0 + jnp.exp(-v))


def conv_cols(ext, seq, start, width, taps, rows):
    total = None
    for tap in range(KERNEL):
        term = taps[tap : tap + 1, start : start + width] * ext[
            seq, pl.ds(8 - (KERNEL - 1) + tap, rows), start : start + width
        ]
        total = term if total is None else total + term
    return total


def lower_masks(rows):
    row = lax.broadcasted_iota(jnp.int32, (rows, rows), 0)
    col = lax.broadcasted_iota(jnp.int32, (rows, rows), 1)
    return row, col


def inverse_many(couplings, row, col):
    rows = row.shape[0]
    eye = (row == col).astype(F32)
    pair = (row // 2 == col // 2)
    out = [eye - jnp.where(pair, a, 0.0) for a in couplings]
    size = 2
    while size < rows:
        mask = (row // (2 * size) == col // (2 * size)) & (row // size != col // size)
        inner = [mm_fine(jnp.where(mask, a, 0.0), t) for a, t in zip(couplings, out)]
        out = [t - mm_fine(t, i) for t, i in zip(out, inner)]
        size *= 2
    return out


def forward_body(
    heads, place, pre, strengths, cols, rows_g, taps, outs, fresh, starts, solved, ext, state
):
    chunk = pl.program_id(0)
    count = pre.shape[3]
    key_all = heads * DK

    @pl.when(chunk == 0)
    def _():
        ext[:, 0:8, :] = jnp.zeros((2, 8, ext.shape[2]), F32)
        state[...] = jnp.zeros(state.shape, F32)

    row, col = lower_masks(count)
    streams = [(seq, head) for seq in range(2) for head in range(heads)]
    for seq in range(2):
        ext[seq, 8 : 8 + count, :] = pre[0, seq, 0].astype(F32)
    queries, keys, values, ratios, couplings = [], [], [], [], []
    for seq, head in streams:
        q = conv_cols(ext, seq, head * DK, DK, taps, count)
        q = q * sigmoid(q)
        q = q * lax.rsqrt(jnp.sum(q * q, axis=1, keepdims=True) + EPS_UNIT)
        k = conv_cols(ext, seq, key_all + head * DK, DK, taps, count)
        k = k * sigmoid(k)
        k = k * lax.rsqrt(jnp.sum(k * k, axis=1, keepdims=True) + EPS_UNIT)
        v = conv_cols(ext, seq, 2 * key_all + head * DV, DV, taps, count)
        v = v * sigmoid(v)
        queries.append(q.astype(BF16))
        keys.append(k.astype(BF16))
        values.append(v.astype(BF16))
        g_col = cols[0, seq, 0, :, 3 * head : 3 * head + 1]
        g_row = rows_g[0, seq, 0, 0, head : head + 1, :]
        ratio = jnp.where(row >= col, jnp.exp(jnp.minimum(g_col - g_row, 0.0)), 0.0)
        ratios.append(ratio)
        beta = sigmoid(strengths[0, seq, 0, :, head : head + 1])
        couplings.append(jnp.where(row > col, beta * ratio * mm_nt(keys[-1], keys[-1]), 0.0))
    for seq in range(2):
        ext[seq, 0:8, :] = ext[seq, count : count + 8, :]
    inverses = inverse_many(couplings, row, col)
    for at, (seq, head) in enumerate(streams):
        q, k, v, ratio = queries[at], keys[at], values[at], ratios[at]
        beta = sigmoid(strengths[0, seq, 0, :, head : head + 1])
        grown = cols[0, seq, 0, :, 3 * head + 1 : 3 * head + 2]
        fade = cols[0, seq, 0, :, 3 * head + 2 : 3 * head + 3]
        held = state[at]
        held_low = held.astype(BF16)
        starts[0, at] = held_low
        inverse = inverses[at].astype(BF16)
        solved[0, at] = inverse
        right = beta * (v.astype(F32) - grown * mm(k, held_low))
        news = mm(inverse, right).astype(BF16)
        scores = ratio * mm_nt(q, k)
        out = mm(scores, news) + grown * mm(q, held_low)
        last = jnp.exp(rows_g[0, seq, 0, 0, head : head + 1, count - 1 : count])
        state[at] = last * held + mm_tn(fade * k.astype(F32), news)
        place_v = slice(head * DV, head * DV + DV)
        fresh[0, seq, 0, :, place_v] = news
        outs[0, seq, 0, :, place_v] = out.astype(BF16)


def backward_body(
    heads,
    place,
    pre,
    halo,
    d_outs,
    d_gate,
    strengths,
    cols,
    rows_g,
    taps,
    fresh,
    starts,
    solved,
    d_all,
    d_taps,
    ext,
    d_ext,
    d_state,
):
    step = pl.program_id(0)
    chunk = pl.num_programs(0) - 1 - step
    count = pre.shape[3]
    key_all = heads * DK

    @pl.when(step == 0)
    def _():
        d_ext[:, count : count + 8, :] = jnp.zeros((2, 8, d_ext.shape[2]), F32)
        d_state[...] = jnp.zeros(d_state.shape, F32)
        d_taps[...] = jnp.zeros(d_taps.shape, F32)

    row, col = lower_masks(count)
    streams = [(seq, head) for seq in range(2) for head in range(heads)]
    keep = jnp.where(chunk > 0, 1.0, 0.0)
    for seq in range(2):
        ext[seq, 0:8, :] = keep * halo[0, seq, 0].astype(F32)[HALO - 8 : HALO, :]
        ext[seq, 8 : 8 + count, :] = pre[0, seq, 0].astype(F32)
    d_betas = []
    for at, (seq, head) in enumerate(streams):
        beta = sigmoid(strengths[0, seq, 0, :, head : head + 1])
        g_col = cols[0, seq, 0, :, 3 * head : 3 * head + 1]
        grown = cols[0, seq, 0, :, 3 * head + 1 : 3 * head + 2]
        fade = cols[0, seq, 0, :, 3 * head + 2 : 3 * head + 3]
        g_row = rows_g[0, seq, 0, 0, head : head + 1, :]
        last = jnp.exp(g_row[:, count - 1 : count])

        q_conv = conv_cols(ext, seq, head * DK, DK, taps, count)
        q_sig = sigmoid(q_conv)
        q_act = q_conv * q_sig
        q_scale = lax.rsqrt(jnp.sum(q_act * q_act, axis=1, keepdims=True) + EPS_UNIT)
        q_unit = q_act * q_scale
        k_conv = conv_cols(ext, seq, key_all + head * DK, DK, taps, count)
        k_sig = sigmoid(k_conv)
        k_act = k_conv * k_sig
        k_scale = lax.rsqrt(jnp.sum(k_act * k_act, axis=1, keepdims=True) + EPS_UNIT)
        k_unit = k_act * k_scale
        v_conv = conv_cols(ext, seq, 2 * key_all + head * DV, DV, taps, count)
        v_sig = sigmoid(v_conv)
        q, k = q_unit.astype(BF16), k_unit.astype(BF16)
        v = (v_conv * v_sig).astype(BF16).astype(F32)
        k_full = k.astype(F32)

        place_v = slice(head * DV, head * DV + DV)
        d_out = d_outs[0, seq, 0, :, place_v]
        news = fresh[0, seq, 0, :, place_v]
        held = starts[0, at]
        inverse = solved[0, at]
        d_held = d_state[at]
        d_held_low = d_held.astype(BF16)
        ratio = jnp.where(row >= col, jnp.exp(jnp.minimum(g_col - g_row, 0.0)), 0.0)
        scores = ratio * mm_nt(q, k)
        d_news = mm_tn(scores, d_out) + mm(fade * k_full, d_held_low)
        d_right = mm_tn(inverse, d_news)
        d_right_low = d_right.astype(BF16)
        d_couple = jnp.where(row > col, -ratio * mm_nt(d_right_low, news), 0.0)
        key_key = mm_nt(k, k)
        d_kk = beta * d_couple
        d_scores = ratio * mm_nt(d_out, news)
        out_held = mm_nt(d_out, held)
        right_held = mm_nt(d_right_low, held)
        news_held = mm_nt(news, d_held_low)
        d_q = mm(d_scores, k) + grown * out_held
        d_k = (
            mm_tn(d_scores, q)
            + mm(d_kk, k)
            + mm_tn(d_kk, k)
            + fade * news_held
            - (beta * grown) * right_held
        )
        d_v = beta * d_right
        d_betas.append(
            jnp.sum(d_right * v, axis=1, keepdims=True)
            - grown * jnp.sum(right_held * k_full, axis=1, keepdims=True)
            + jnp.sum(d_couple * key_key, axis=1, keepdims=True)
        )
        d_state[at] = (
            last * d_held
            + mm_tn(grown * q.astype(F32), d_out)
            - mm_tn((beta * grown) * k_full, d_right_low)
        )
        d_qa = q_scale * (d_q - q_unit * jnp.sum(q_unit * d_q, axis=1, keepdims=True))
        d_ka = k_scale * (d_k - k_unit * jnp.sum(k_unit * d_k, axis=1, keepdims=True))
        d_ext[seq, 0:count, head * DK : head * DK + DK] = d_qa * (
            q_sig * (1.0 + q_conv * (1.0 - q_sig))
        )
        d_ext[seq, 0:count, key_all + head * DK : key_all + head * DK + DK] = d_ka * (
            k_sig * (1.0 + k_conv * (1.0 - k_sig))
        )
        d_ext[
            seq, 0:count, 2 * key_all + head * DV : 2 * key_all + head * DV + DV
        ] = d_v * (v_sig * (1.0 + v_conv * (1.0 - v_sig)))
    for seq in range(2):
        lane = lax.broadcasted_iota(jnp.int32, (count, BETA_LANES), 1)
        d_beta = jnp.zeros((count, BETA_LANES), F32)
        for head in range(heads):
            beta = sigmoid(strengths[0, seq, 0, :, head : head + 1])
            d_beta = jnp.where(
                lane == head, d_betas[seq * heads + head] * beta * (1.0 - beta), d_beta
            )
        wide = ext.shape[2]
        d_all[0, seq, 0, :, wide : wide + BETA_LANES] = d_beta.astype(BF16)
        d_all[0, seq, 0, :, wide + BETA_LANES :] = d_gate[0, seq, 0]
        for start in range(0, wide, 128):
            span = slice(start, start + 128)
            total = None
            near = d_ext[seq, 0:count, span]
            for tap in range(KERNEL):
                term = taps[tap : tap + 1, span] * d_ext[seq, pl.ds(KERNEL - 1 - tap, count), span]
                total = term if total is None else total + term
                moved = ext[seq, pl.ds(8 - (KERNEL - 1) + tap, count), span]
                d_taps[tap : tap + 1, span] += jnp.sum(near * moved, axis=0, keepdims=True)
            d_all[0, seq, 0, :, span] = total.astype(BF16)
        d_ext[seq, count : count + 8, :] = d_ext[seq, 0:8, :]


def chunk_block(chunk, place, per_piece):
    piece = jnp.bitwise_xor(chunk // per_piece, place[0])
    return piece % 2, piece // 2, chunk % per_piece


def chunk_specs(turn, per_piece):
    def by_rows(width):
        def index(step, at):
            half, piece, within = chunk_block(turn(step), at, per_piece)
            return (half, 0, piece, within, 0)

        return pl.BlockSpec((1, 2, 1, CHUNK, width), index)

    def by_chunk(heads):
        def index(step, at):
            half, piece, within = chunk_block(turn(step), at, per_piece)
            return (half, 0, piece, within, 0, 0)

        return pl.BlockSpec((1, 2, 1, 1, heads, CHUNK), index)

    return by_rows, by_chunk


def run_forward(place, pre, strengths, cols, rows_g, taps):
    halves, _, pieces, piece_rows, wide = pre.shape
    heads = rows_g.shape[-2]
    per_piece = piece_rows // CHUNK
    chunks = halves * pieces * per_piece
    by_rows, by_chunk = chunk_specs(lambda step: step, per_piece)
    grid_spec = pltpu.PrefetchScalarGridSpec(
        num_scalar_prefetch=1,
        grid=(chunks,),
        in_specs=[
            by_rows(wide),
            by_rows(BETA_LANES),
            by_rows(3 * heads),
            by_chunk(heads),
            pl.BlockSpec((8, wide), lambda c, at: (0, 0)),
        ],
        out_specs=[
            by_rows(heads * DV),
            by_rows(heads * DV),
            pl.BlockSpec((1, 2 * heads, DK, DV), lambda c, at: (c, 0, 0, 0)),
            pl.BlockSpec((1, 2 * heads, CHUNK, CHUNK), lambda c, at: (c, 0, 0, 0)),
        ],
        scratch_shapes=[
            pltpu.VMEM((2, CHUNK + 8, wide), F32),
            pltpu.VMEM((2 * heads, DK, DV), F32),
        ],
    )
    rows_out = jax.ShapeDtypeStruct(pre.shape[:-1] + (heads * DV,), BF16)
    return pl.pallas_call(
        functools.partial(forward_body, heads),
        grid_spec=grid_spec,
        out_shape=[
            rows_out,
            rows_out,
            jax.ShapeDtypeStruct((chunks, 2 * heads, DK, DV), BF16),
            jax.ShapeDtypeStruct((chunks, 2 * heads, CHUNK, CHUNK), BF16),
        ],
        compiler_params=VMEM_PARAMS,
        name="delta_forward",
    )(place, pre, strengths, cols, rows_g, taps)


def run_backward(
    place, pre, d_outs, d_gate, strengths, cols, rows_g, taps, fresh, starts, solved
):
    halves, _, pieces, piece_rows, wide = pre.shape
    heads = d_outs.shape[-1] // DV
    per_piece = piece_rows // CHUNK
    chunks = halves * pieces * per_piece
    per_halo = CHUNK // HALO
    wide_out = wide + BETA_LANES + heads * DV

    def turned(step):
        return chunks - 1 - step

    by_rows, by_chunk = chunk_specs(turned, per_piece)

    def halo_place(step, at):
        half, piece, within = chunk_block(jnp.maximum(turned(step) - 1, 0), at, per_piece)
        return (half, 0, piece, within * per_halo + per_halo - 1, 0)

    grid_spec = pltpu.PrefetchScalarGridSpec(
        num_scalar_prefetch=1,
        grid=(chunks,),
        in_specs=[
            by_rows(wide),
            pl.BlockSpec((1, 2, 1, HALO, wide), halo_place),
            by_rows(heads * DV),
            by_rows(heads * DV),
            by_rows(BETA_LANES),
            by_rows(3 * heads),
            by_chunk(heads),
            pl.BlockSpec((8, wide), lambda c, at: (0, 0)),
            by_rows(heads * DV),
            pl.BlockSpec((1, 2 * heads, DK, DV), lambda c, at: (turned(c), 0, 0, 0)),
            pl.BlockSpec((1, 2 * heads, CHUNK, CHUNK), lambda c, at: (turned(c), 0, 0, 0)),
        ],
        out_specs=[by_rows(wide_out), pl.BlockSpec((8, wide), lambda c, at: (0, 0))],
        scratch_shapes=[
            pltpu.VMEM((2, CHUNK + 8, wide), F32),
            pltpu.VMEM((2, CHUNK + 8, wide), F32),
            pltpu.VMEM((2 * heads, DK, DV), F32),
        ],
    )
    return pl.pallas_call(
        functools.partial(backward_body, heads),
        grid_spec=grid_spec,
        out_shape=[
            jax.ShapeDtypeStruct(pre.shape[:-1] + (wide_out,), BF16),
            jax.ShapeDtypeStruct((8, wide), F32),
        ],
        compiler_params=VMEM_PARAMS,
        name="delta_backward",
    )(place, pre, pre, d_outs, d_gate, strengths, cols, rows_g, taps, fresh, starts, solved)


def norm_body(half, other, scale, gain, out):
    step = pl.program_id(0)

    @pl.when(step < pl.num_programs(0) // 2)
    def _():
        out[...] = (half[...].astype(F32) * scale[...] * gain[...]).astype(BF16)

    @pl.when(step >= pl.num_programs(0) // 2)
    def _():
        out[...] = (other[...].astype(F32) * scale[...] * gain[...]).astype(BF16)


def run_norm(half, other, scale, gain):
    length, model = half.shape
    tile = 256
    steps = length // tile
    return pl.pallas_call(
        norm_body,
        grid=(2 * steps,),
        in_specs=[
            pl.BlockSpec((tile, model), lambda i: (jnp.minimum(i, steps - 1), 0)),
            pl.BlockSpec((tile, model), lambda i: (jnp.maximum(i - steps, 0), 0)),
            pl.BlockSpec((tile, 1), lambda i: (i, 0)),
            pl.BlockSpec((1, model), lambda i: (0, 0)),
        ],
        out_specs=pl.BlockSpec((tile, model), lambda i: (i, 0)),
        out_shape=jax.ShapeDtypeStruct((2 * length, model), BF16),
        compiler_params=VMEM_PARAMS,
        name="norm_rows",
    )(half, other, scale, gain)


def place_rows(pieces, places, out, gain=None):
    for piece, start, size, target in places:
        rows = pieces[piece][start : start + size, :]
        if gain is not None:
            rows = (rows.astype(F32) * gain[...]).astype(BF16)
        out[target : target + size, :] = rows


def project_body(count, places, narrow, half, other, gain, scale, *refs):
    pieces, weights, outs = refs[:count], refs[count], refs[count + 1 :]
    step, steps = pl.program_id(0), pl.num_programs(0) // 2

    @pl.when(step == 0)
    def _():
        place_rows(pieces, places, weights, gain)

    for chosen, tokens in ((step < steps, half), (step >= steps, other)):

        @pl.when(chosen)
        def _():
            sums = mm_nt(tokens[...], weights[...]) * scale[...]
            outs[0][...] = sums[:, :narrow].astype(BF16)
            if len(outs) > 1:
                outs[1][...] = sums[:, narrow:]


def whole_block(shape):
    return pl.BlockSpec(shape, lambda i: (0, 0), pipeline_mode=pl.Buffered(1))


def run_project(halves, pieces, places, gain, scale, wide, narrow):
    length, model = halves[0].shape
    tile = 256
    steps = length // tile
    out_shape = [jax.ShapeDtypeStruct((wide, model), BF16)]
    out_shape.append(jax.ShapeDtypeStruct((2 * length, narrow), BF16))
    if wide > narrow:
        out_shape.append(jax.ShapeDtypeStruct((2 * length, wide - narrow), F32))
    return pl.pallas_call(
        functools.partial(project_body, len(pieces), places, narrow),
        grid=(2 * steps,),
        in_specs=[
            pl.BlockSpec((tile, model), lambda i: (jnp.minimum(i, steps - 1), 0)),
            pl.BlockSpec((tile, model), lambda i: (jnp.maximum(i - steps, 0), 0)),
            whole_block((1, model)),
            pl.BlockSpec((tile, 1), lambda i: (i, 0)),
        ]
        + [whole_block(piece.shape) for piece in pieces],
        out_specs=[pl.BlockSpec((wide, model), lambda i: (0, 0))]
        + [pl.BlockSpec((tile, one.shape[1]), lambda i: (i, 0)) for one in out_shape[1:]],
        out_shape=out_shape,
        compiler_params=VMEM_PARAMS,
        name="project_rows",
    )(*halves, gain, scale, *pieces)


def hidden_body(count, feed_places, down_places, first, second, *refs):
    pieces, (feed_rows, down_rows, back_first, back_second) = refs[:count], refs[count:]
    step, steps = pl.program_id(0), pl.num_programs(0) // 2

    @pl.when(step == 0)
    def _():
        place_rows(pieces, feed_places, feed_rows)
        place_rows(pieces, down_places, down_rows)

    for chosen, grads, back in (
        (step < steps, first, back_first),
        (step >= steps, second, back_second),
    ):

        @pl.when(chosen)
        def _():
            back[...] = mm_nt(down_rows[...], grads[...]).astype(BF16)


def run_hidden(grads, pieces, feed_places, down_places, units):
    length, model = grads[0].shape
    tile = 256
    steps = length // tile
    return pl.pallas_call(
        functools.partial(hidden_body, len(pieces), feed_places, down_places),
        grid=(2 * steps,),
        in_specs=[
            pl.BlockSpec((tile, model), lambda i: (jnp.minimum(i, steps - 1), 0)),
            pl.BlockSpec((tile, model), lambda i: (jnp.maximum(i - steps, 0), 0)),
        ]
        + [whole_block(piece.shape) for piece in pieces],
        out_specs=[
            pl.BlockSpec((2 * units, model), lambda i: (0, 0)),
            pl.BlockSpec((units, model), lambda i: (0, 0)),
            pl.BlockSpec((units, tile), lambda i: (0, jnp.minimum(i, steps - 1))),
            pl.BlockSpec((units, tile), lambda i: (0, jnp.maximum(i - steps, 0))),
        ],
        out_shape=[
            jax.ShapeDtypeStruct((2 * units, model), BF16),
            jax.ShapeDtypeStruct((units, model), BF16),
            jax.ShapeDtypeStruct((units, length), BF16),
            jax.ShapeDtypeStruct((units, length), BF16),
        ],
        compiler_params=VMEM_PARAMS,
        name="hidden_cotangents",
    )(*grads, *pieces)


def feed_body(feed, weights, back, hidden, d_both, d_feed):
    units = back.shape[0]
    rows = feed[...]
    gate = mm_nt(weights[:units, :], rows)
    up = mm_nt(weights[units:, :], rows)
    sig = sigmoid(gate)
    smooth = gate * sig
    d_hidden = back[...].astype(F32)
    hidden[...] = (smooth * up).astype(BF16)
    d_gate = (d_hidden * up * (sig * (1.0 + gate * (1.0 - sig)))).astype(BF16)
    d_up = (d_hidden * smooth).astype(BF16)
    d_both[:units, :] = d_gate
    d_both[units:, :] = d_up
    d_feed[...] = (
        mm_tn(d_gate, weights[:units, :]) + mm_tn(d_up, weights[units:, :])
    ).astype(BF16)


def run_feed(feed, weights, back):
    length, model = feed.shape
    units = back.shape[0]
    tile = 256
    return pl.pallas_call(
        feed_body,
        grid=(length // tile,),
        in_specs=[
            pl.BlockSpec((tile, model), lambda i: (i, 0)),
            pl.BlockSpec((2 * units, model), lambda i: (0, 0)),
            pl.BlockSpec((units, tile), lambda i: (0, i)),
        ],
        out_specs=[
            pl.BlockSpec((units, tile), lambda i: (0, i)),
            pl.BlockSpec((2 * units, tile), lambda i: (0, i)),
            pl.BlockSpec((tile, model), lambda i: (i, 0)),
        ],
        out_shape=[
            jax.ShapeDtypeStruct((units, length), BF16),
            jax.ShapeDtypeStruct((2 * units, length), BF16),
            jax.ShapeDtypeStruct((length, model), BF16),
        ],
        compiler_params=VMEM_PARAMS,
        name="feed_forward",
    )(feed, weights, back)


def outer_body(first, second, right_first, right_second, out):
    out[...] = (
        mm(first[...], right_first[...]) + mm(second[...], right_second[...])
    ).astype(BF16)


def run_outer(lefts, rights):
    wide, length = lefts[0].shape
    model = rights[0].shape[1]
    tile = 176 if wide % 176 == 0 else wide
    left = pl.BlockSpec((tile, length), lambda i: (i, 0))
    right = pl.BlockSpec((length, model), lambda i: (0, 0))
    return pl.pallas_call(
        outer_body,
        grid=(wide // tile,),
        in_specs=[left, left, right, right],
        out_specs=pl.BlockSpec((tile, model), lambda i: (i, 0)),
        out_shape=jax.ShapeDtypeStruct((wide, model), BF16),
        compiler_params=VMEM_PARAMS,
        name="outer_sums",
    )(*lefts, *rights)


def back_body(d_rows, weights, normed, out, gain):
    @pl.when(pl.program_id(0) == 0)
    def _():
        gain[...] = jnp.zeros(gain.shape, F32)

    sums = mm(d_rows[...], weights[...])
    out[...] = sums.astype(BF16)
    gain[0:1, :] += jnp.sum(sums * normed[...].astype(F32), axis=0, keepdims=True)


def run_back(d_rows, weights, normed, half):
    length, wide = d_rows.shape[0] // 2, d_rows.shape[1]
    model = weights.shape[1]
    tile = 256
    start = half * (length // tile)
    return pl.pallas_call(
        back_body,
        grid=(length // tile,),
        in_specs=[
            pl.BlockSpec((tile, wide), lambda i: (start + i, 0)),
            pl.BlockSpec((wide, model), lambda i: (0, 0)),
            pl.BlockSpec((tile, model), lambda i: (start + i, 0)),
        ],
        out_specs=[
            pl.BlockSpec((tile, model), lambda i: (i, 0)),
            pl.BlockSpec((8, model), lambda i: (0, 0)),
        ],
        out_shape=[
            jax.ShapeDtypeStruct((length, model), BF16),
            jax.ShapeDtypeStruct((8, model), F32),
        ],
        compiler_params=VMEM_PARAMS,
        name="back_rows",
    )(d_rows, weights, normed)


def weigh_body(parts, d_rows, normed, taps, out):
    count, key_part, value_part = parts
    step = pl.program_id(0)
    piece = 2 * key_part + value_part + 16
    sums = mm_tn(d_rows[...], normed[...]).astype(BF16)
    tile = sums.shape[0]
    key_steps = count * key_part // tile
    value_steps = count * value_part // tile

    def store(part, first_step, offset):
        for at in range(tile // part):
            target = (step - first_step) * (tile // part) + at
            start = pl.multiple_of(target * piece + offset, 16)
            out[pl.ds(start, part), :] = sums[at * part : (at + 1) * part, :]

    @pl.when(step < key_steps)
    def _():
        store(key_part, 0, 0)

    @pl.when((step >= key_steps) & (step < 2 * key_steps))
    def _():
        store(key_part, key_steps, key_part)

    @pl.when((step >= 2 * key_steps) & (step < 2 * key_steps + value_steps))
    def _():
        store(value_part, 2 * key_steps, 2 * key_part)

    @pl.when(step == 2 * key_steps + value_steps)
    def _():
        out[count * piece : count * piece + tile, :] = sums
        for at in range(count):
            start = at * piece + piece - 16
            out[start : start + 16, :] = taps[at * 16 : at * 16 + 16, :]


def run_weigh(d_rows, normed, taps, parts):
    count, key_part, value_part = parts
    length = d_rows.shape[0]
    model = normed.shape[1]
    tile = 128
    wide = count * (2 * key_part + value_part)
    rows = wide + 16 * count + tile
    return pl.pallas_call(
        functools.partial(weigh_body, parts),
        grid=(wide // tile + 1,),
        in_specs=[
            pl.BlockSpec((length, tile), lambda i: (0, i)),
            whole_block((length, model)),
            whole_block(taps.shape),
        ],
        out_specs=pl.BlockSpec((rows, model), lambda i: (0, 0)),
        out_shape=jax.ShapeDtypeStruct((rows, model), BF16),
        compiler_params=VMEM_PARAMS,
        name="weight_sums",
    )(d_rows, normed, taps)


def mixer_back_body(
    heads,
    part,
    branch_own,
    branch_other,
    out_rows,
    head_outs,
    gate_own,
    gate_other,
    mixed_own,
    mixed_other,
    normed,
    gain,
    d_outs,
    d_gate,
    d_gain,
    terms,
    out_sums,
    gate_sums,
):
    step, steps = pl.program_id(0), pl.num_programs(0) // 2

    @pl.when(step == 0)
    def _():
        d_gain[...] = jnp.zeros(d_gain.shape, F32)
        out_sums[...] = jnp.zeros(out_sums.shape, F32)
        gate_sums[...] = jnp.zeros(gate_sums.shape, F32)

    for chosen, branch, gate, mixed in (
        (step < steps, branch_own, gate_own, mixed_own),
        (step >= steps, branch_other, gate_other, mixed_other),
    ):

        @pl.when(chosen)
        def _():
            d_mixed = mm_nt(branch[...], out_rows[...])
            out_sums[...] += mm_tn(mixed[...], branch[...])
            total = None
            for head in range(heads):
                span = slice(head * DV, head * DV + DV)
                out = head_outs[:, span].astype(F32)
                grad = d_mixed[:, span]
                g = gate[:, span].astype(F32)
                sig = sigmoid(g)
                scale = lax.rsqrt(jnp.mean(out * out, axis=1, keepdims=True) + EPS_NORM)
                unit = out * scale
                cot = grad * (g * sig)
                term = jnp.sum(cot * unit, axis=0, keepdims=True)
                total = term if total is None else total + term
                scaled = cot * gain[0:1, :]
                d_outs[:, span] = (
                    scale * (scaled - unit * jnp.mean(unit * scaled, axis=1, keepdims=True))
                ).astype(BF16)
                d_gate[:, span] = (
                    grad * unit * gain[0:1, :] * (sig * (1.0 + g * (1.0 - sig)))
                ).astype(BF16)
            d_gain[0:1, :] += total
            gate_sums[...] += mm_tn(d_gate[...], normed[...])

    @pl.when(step == 2 * steps - 1)
    def _():
        for at in range(out_sums.shape[0] // part):
            span = slice(at * part, (at + 1) * part)
            start = 2 * at * part
            terms[start : start + part, :] = gate_sums[span, :].astype(BF16)
            terms[start + part : start + 2 * part, :] = out_sums[span, :].astype(BF16)


def run_mixer_back(branches, out_rows, head_outs, gates, mixed, normed, gain, part):
    length, model = branches[0].shape
    wide = out_rows.shape[0]
    tile = 512
    steps = length // tile
    rows = pl.BlockSpec((tile, wide), lambda i: (i, 0))
    first = pl.BlockSpec((tile, wide), lambda i: (jnp.minimum(i, steps - 1), 0))
    second = pl.BlockSpec((tile, wide), lambda i: (jnp.maximum(i - steps, 0), 0))
    sums = pl.BlockSpec((2 * wide, model), lambda i: (0, 0))
    return pl.pallas_call(
        functools.partial(mixer_back_body, wide // DV, part),
        grid=(2 * steps,),
        in_specs=[
            pl.BlockSpec((tile, model), lambda i: (jnp.minimum(i, steps - 1), 0)),
            pl.BlockSpec((tile, model), lambda i: (jnp.maximum(i - steps, 0), 0)),
            whole_block((wide, model)),
            rows,
            first,
            second,
            first,
            second,
            pl.BlockSpec((tile, model), lambda i: (i, 0)),
            pl.BlockSpec((1, DV), lambda i: (0, 0)),
        ],
        out_specs=[rows, rows, pl.BlockSpec((8, DV), lambda i: (0, 0)), sums],
        out_shape=[
            jax.ShapeDtypeStruct((2 * length, wide), BF16),
            jax.ShapeDtypeStruct((2 * length, wide), BF16),
            jax.ShapeDtypeStruct((8, DV), F32),
            jax.ShapeDtypeStruct((2 * wide, model), BF16),
        ],
        scratch_shapes=[pltpu.VMEM((wide, model), F32), pltpu.VMEM((wide, model), F32)],
        compiler_params=VMEM_PARAMS,
        name="mixer_backward",
    )(*branches, out_rows, head_outs, *gates, *mixed, normed, gain)


def branch_body(count, gate_places, out_places, heads, tokens, gain, scale, head_outs, head_gain, *refs):
    pieces, (gate_rows, out_rows, gate, mixed, branch) = refs[:count], refs[count:]

    @pl.when(pl.program_id(0) == 0)
    def _():
        place_rows(pieces, gate_places, gate_rows, gain)
        place_rows(pieces, out_places, out_rows)

    gate_pre = mm_nt(tokens[...], gate_rows[...]) * scale[...]
    gate[...] = gate_pre.astype(BF16)
    for head in range(heads):
        span = slice(head * DV, head * DV + DV)
        out = head_outs[:, span].astype(F32)
        factor = lax.rsqrt(jnp.mean(out * out, axis=1, keepdims=True) + EPS_NORM)
        g = gate_pre[:, span]
        mixed[:, span] = (out * factor * head_gain[0:1, :] * (g * sigmoid(g))).astype(BF16)
    branch[...] = mm(mixed[...], out_rows[...]).astype(BF16)


def run_branch(half, tokens, pieces, gate_places, out_places, gain, scale, head_outs, head_gain):
    length, model = tokens.shape
    wide = head_outs.shape[1]
    tile = 256
    start = half * (length // tile)
    rows = pl.BlockSpec((tile, wide), lambda i: (i, 0))
    weights = pl.BlockSpec((wide, model), lambda i: (0, 0))
    return pl.pallas_call(
        functools.partial(branch_body, len(pieces), gate_places, out_places, wide // DV),
        grid=(length // tile,),
        in_specs=[
            pl.BlockSpec((tile, model), lambda i: (i, 0)),
            whole_block((1, model)),
            pl.BlockSpec((tile, 1), lambda i: (start + i, 0)),
            pl.BlockSpec((tile, wide), lambda i: (start + i, 0)),
            pl.BlockSpec((1, DV), lambda i: (0, 0)),
        ]
        + [whole_block(piece.shape) for piece in pieces],
        out_specs=[
            weights,
            weights,
            rows,
            rows,
            pl.BlockSpec((tile, model), lambda i: (i, 0)),
        ],
        out_shape=[
            jax.ShapeDtypeStruct((wide, model), BF16),
            jax.ShapeDtypeStruct((wide, model), BF16),
            jax.ShapeDtypeStruct((length, wide), BF16),
            jax.ShapeDtypeStruct((length, wide), BF16),
            jax.ShapeDtypeStruct((length, model), BF16),
        ],
        compiler_params=VMEM_PARAMS,
        name="branch_rows",
    )(tokens, gain, scale, head_outs, head_gain, *pieces)


def finish_body(count, outputs, *refs):
    given, outs = refs[:count], refs[count:]
    for (segments, turned), out in zip(outputs, outs):
        slabs = []
        for size, sources in segments:
            total = None
            for which, start in sources:
                term = given[which][start : start + size, :].astype(F32)
                total = term if total is None else total + term
            slabs.append(total)
        slab = slabs[0] if len(slabs) == 1 else jnp.concatenate(slabs, axis=0)
        if turned:
            rows = slab.shape[0]
            spare = -rows % 128
            if spare:
                slab = jnp.concatenate([slab, jnp.zeros((spare, slab.shape[1]), F32)], axis=0)
            out[...] = slab.T[:, :rows]
        else:
            out[...] = slab


def run_finish(given, outputs):
    model = given[0].shape[1]
    tile = 256
    out_specs, out_shape = [], []
    for segments, turned in outputs:
        rows = sum(size for size, _ in segments)
        if turned:
            out_specs.append(pl.BlockSpec((tile, rows), lambda i: (i, 0)))
            out_shape.append(jax.ShapeDtypeStruct((model, rows), F32))
        else:
            out_specs.append(pl.BlockSpec((rows, tile), lambda i: (0, i)))
            out_shape.append(jax.ShapeDtypeStruct((rows, model), F32))
    return pl.pallas_call(
        functools.partial(finish_body, len(given), outputs),
        grid=(model // tile,),
        in_specs=[pl.BlockSpec((piece.shape[0], tile), lambda i: (0, i)) for piece in given],
        out_specs=out_specs,
        out_shape=out_shape,
        compiler_params=VMEM_PARAMS,
        name="finish_sums",
    )(*given)


def product(left_side, right_side):
    return jnp.dot(left_side, right_side, preferred_element_type=F32)


def product_tn(left_side, right_side):
    return lax.dot_general(
        left_side, right_side, (((0,), (0,)), ((), ())), preferred_element_type=F32
    )


def product_nt(left_side, right_side):
    return lax.dot_general(
        left_side, right_side, (((1,), (1,)), ((), ())), preferred_element_type=F32
    )


def rms_scale(values, gain_vals):
    return (
        values * lax.rsqrt(jnp.mean(values * values, axis=-1, keepdims=True) + EPS_NORM) * gain_vals
    )


def swap(values, axis, bit):
    count = lax.axis_size(axis)
    return lax.ppermute(values, axis, [(place, place ^ bit) for place in range(count)])


def bits_of(count):
    found = []
    bit = 1
    while bit < count:
        found.append(bit)
        bit *= 2
    return found


def after(values, *earlier):
    return lax.optimization_barrier((values, *earlier))[0]


def add_low(left_side, right_side):
    return (left_side.astype(F32) + right_side.astype(F32)).astype(BF16)


def along_x(first):
    count = lax.axis_size("seq") // 2
    pieces = {0: first}
    for offset in sorted(range(1, count), key=lambda o: (-(o & -o), o)):
        low = offset & -offset
        pieces[offset] = swap(pieces[offset ^ low], "seq", 2 * low)
    return [pieces[offset] for offset in range(count)]


def fold_rows(part_own, part_other):
    return fold_came(part_own, swap(part_other, "seq", 1))


def fold_came(part_own, came):
    count = lax.axis_size("seq") // 2
    rows = part_own.shape[0] // (2 * count)
    folded = []
    for start in (count, 0):
        pieces = {}
        for at in reversed(range(count)):
            span = slice((start + at) * rows, (start + at + 1) * rows)
            pieces[at] = add_low(part_own[span], came[span])
        folded.append(pieces)
    return folded


def send_along(pieces):
    return {at: swap(piece, "seq", 2 * at) for at, piece in pieces.items() if at}


def add_along(pieces, came):
    return sum(
        [piece.astype(F32) for piece in came.values()], pieces[0].astype(F32)
    ).astype(BF16)


def cut(values, at, size):
    return values[at * size : (at + 1) * size]


def send_bits(pieces, axis, chosen):
    at = 1 if axis == "low" else 0
    return {
        offset: swap(pieces[offset], axis, offset[at]) for offset in chosen if offset[at]
    }


def add_bits(pieces, came, hold=()):
    pieces = dict(pieces)
    for offset, piece in came.items():
        pieces.pop(offset)
        target = (offset[0], 0)
        kept = after(pieces[target], *hold) if hold else pieces[target]
        total = kept.astype(F32) + piece.astype(F32)
        pieces[target] = total if target == (0, 0) else total.astype(BF16)
    return pieces


def sum_pieces(pieces, near, far):
    return sum(
        [piece.astype(F32) for piece in (*near.values(), *far.values())],
        pieces[0, 0].astype(F32),
    )


def spread_stage(values, axis, bits=None):
    for bit in bits_of(lax.axis_size(axis)) if bits is None else bits:
        came = swap(values, axis, bit)
        values = jnp.where(
            (lax.axis_index(axis) & bit) == 0,
            jnp.concatenate([values, came], axis=0),
            jnp.concatenate([came, values], axis=0),
        )
    return values


def sum_stage(values, axis, dim, bits=None):
    for bit in reversed(bits_of(lax.axis_size(axis)) if bits is None else bits):
        lower, upper = jnp.split(values, 2, axis=dim)
        is_upper = (lax.axis_index(axis) & bit) != 0
        kept = jnp.where(is_upper, upper, lower)
        values = kept + swap(jnp.where(is_upper, lower, upper), axis, bit)
    return values


def local(
    tokens,
    decays,
    out_grad,
    mixer_gain,
    query_weight,
    key_weight,
    value_weight,
    beta_weight,
    outgate_weight,
    query_conv,
    key_conv,
    value_conv,
    head_gain,
    output_weight,
    feed_gain,
    feed_gate,
    feed_up,
    feed_down,
):
    seq_count = lax.axis_size("seq")
    high_count = lax.axis_size("high")
    low_count = lax.axis_size("low")
    seq_pos = lax.axis_index("seq")
    low_pos = lax.axis_index("low")
    devices = seq_count * high_count * 2 * low_count
    heads = high_count
    source = tokens[0]
    grad_own = out_grad[0]
    rows, model = source.shape
    length = rows * seq_count
    pieces_x = seq_count // 2
    key_part = query_weight.shape[1]
    value_part = value_weight.shape[1]
    feed_part = feed_gate.shape[1]
    gain_part = mixer_gain.shape[0]
    head_part = head_gain.shape[0]
    offsets = [(high, low) for high in range(high_count) for low in range(low_count)]
    count = len(offsets)
    far_offsets = [o for o in offsets if o[0] and not o[1]]
    near_offsets = [o for o in offsets if not o[0] and o[1]]
    cross_offsets = [o for o in offsets if o[0] and o[1]]

    groups = []

    def settle(*values):
        places = [(got, offset) for got in groups for offset in got]
        values, pieces = lax.optimization_barrier(
            (values, [got[offset] for got, offset in places])
        )
        for (got, offset), piece in zip(places, pieces):
            got[offset] = piece
        return values

    def fetch(got, chosen):
        if not got[0, 0].shape[0]:
            return
        for high, low in sorted(chosen, key=lambda o: (o[0], -(o[1] & -o[1]), o[1])):
            if low == 0:
                axis, bit, start = "high", high & -high, (high ^ (high & -high), 0)
            else:
                axis, bit, start = "low", low & -low, (high, low ^ (low & -low))
            got[high, low] = swap(got[start], axis, bit)

    def joined(got, start, size):
        return [got[offset][start : start + size] for offset in offsets]

    source_f = source.astype(F32)
    scale_own = lax.rsqrt(jnp.mean(source_f * source_f, axis=-1, keepdims=True) + EPS_NORM)
    small = jnp.concatenate([mixer_gain, feed_gain, beta_weight.T.reshape(-1), head_gain], axis=0)
    small_size = small.shape[0]
    small = jnp.pad(small, (0, -small_size % 2048)).reshape(1, -1, 128)
    small = spread_stage(small, "high")
    small = spread_stage(small, "low")
    small = spread_stage(small, "team")
    logs = jnp.concatenate([jnp.log(decays[0]), scale_own.reshape(1, rows)], axis=0)
    logs = jnp.pad(logs, ((0, -logs.shape[0] % 8), (0, 0)))
    logs = jnp.stack([logs, swap(logs, "team", 1)], axis=0)[:, None]
    taps_own = jnp.concatenate([query_conv, key_conv, value_conv], axis=1)
    taps_wide = taps_own.shape[1]
    taps_rows = jnp.pad(taps_own, ((0, 16 - KERNEL), (0, model - taps_wide)))
    head_got = {(0, 0): jnp.concatenate([query_weight.T, key_weight.T], axis=0)}
    value_got = {(0, 0): jnp.concatenate([value_weight.T, taps_rows], axis=0)}
    groups += [head_got]
    source_x = along_x(source)
    small, logs, source_kept, grad_kept = settle(small, logs, source, grad_own)

    source_team = swap(source_kept, "team", 1)
    fetch(head_got, far_offsets)
    fetch(head_got, near_offsets)
    groups += [value_got]
    small = spread_stage(small, "seq", (1,))
    small = spread_stage(after(small, source_x[-1]), "seq", bits_of(seq_count)[1:])
    for bit in bits_of(seq_count)[1:]:
        logs = jnp.concatenate([logs, swap(after(logs, source_x[-1]), "seq", bit)], axis=1)
    logs = jnp.stack([logs, swap(logs, "seq", 1)], axis=0)
    small, logs, source_x, source_team = settle(small, logs, source_x, source_team)

    team_x = along_x(source_team)
    fetch(value_got, far_offsets)
    fetch(head_got, cross_offsets)
    fetch(value_got, near_offsets)
    gate_got = {(0, 0): outgate_weight.T}
    out_got = {(0, 0): output_weight}
    groups += [gate_got, out_got]
    small_all = small.reshape((seq_count, 2, low_count, high_count, -1)).transpose(0, 3, 1, 2, 4)
    small_all = small_all.reshape(devices, -1)
    gain_f = small_all[:, :gain_part].reshape(-1).astype(F32)
    feed_gain_f = small_all[:, gain_part : 2 * gain_part].reshape(-1).astype(F32)
    beta_rows = (
        small_all[:, 2 * gain_part : 2 * gain_part + H * gain_part]
        .reshape(devices, H, gain_part)
        .transpose(1, 0, 2)
        .reshape(H, model)
    )
    head_gain_all = small_all[:, small_size - head_part : small_size].reshape(-1)
    gain_blocks = head_gain_all.reshape(low_count, DV // low_count)
    gain_row = jnp.concatenate(
        [
            lax.dynamic_index_in_dim(gain_blocks, at ^ low_pos, 0, False)
            for at in range(low_count)
        ],
        axis=0,
    ).astype(F32)[None]
    head_places = [
        seq_pos * (2 * heads) + 2 * (lax.axis_index("high") ^ head) + lax.axis_index("team")
        for head in range(heads)
    ]
    beta_own = jnp.stack(
        [lax.dynamic_index_in_dim(beta_rows, place, 0, False) for place in head_places], axis=0
    )

    head_logs = jnp.stack(
        [lax.dynamic_index_in_dim(logs, place, 3, False) for place in head_places], axis=3
    )
    outer = (2, 2, pieces_x)
    scale_all = logs[:, :, :, H].reshape(2 * length, 1)
    per_piece = rows // CHUNK
    totals = jnp.cumsum(head_logs.reshape(outer + (heads, per_piece, CHUNK)), axis=-1)
    rows_g = totals.transpose(0, 1, 2, 4, 3, 5)

    def as_cols(values):
        return values.transpose(0, 1, 2, 4, 5, 3).reshape(outer + (rows, heads))

    totals_cols = as_cols(totals)
    fade_cols = as_cols(jnp.exp(totals[..., -1:] - totals))

    half_tokens = jnp.concatenate(list(source_x) + list(team_x), axis=0)
    (
        half_tokens,
        grad_kept,
        gain_f,
        feed_gain_f,
        beta_own,
        gain_row,
        scale_all,
        rows_g,
        cols,
        beta_block,
    ) = settle(
        half_tokens,
        grad_kept,
        gain_f,
        feed_gain_f,
        beta_own,
        gain_row,
        scale_all,
        rows_g,
        jnp.stack([totals_cols, jnp.exp(totals_cols), fade_cols], axis=-1).reshape(
            outer + (rows, 3 * heads)
        ),
        jnp.pad(beta_own, ((0, BETA_LANES - heads), (0, 0))),
    )

    other_tokens = swap(half_tokens, "seq", 1)
    fetch(value_got, cross_offsets)
    fetch(gate_got, far_offsets)

    ends = [feed_part * part // 11 // 16 * 16 for part in (3, 4, 6, 9)] + [feed_part]
    starts_at = [0] + ends[:-1]
    units = [end - start for start, end in zip(starts_at, ends)]
    first_count = ends[2]
    shares = []
    for start, end in zip(starts_at, ends):
        span = slice(start, end)
        shares.append(
            jnp.concatenate([feed_gate[:, span].T, feed_up[:, span].T, feed_down[span]], axis=0)
        )
    fine_gots = [{(0, 0): share} for share in shares]
    coarse_ranges = ((0,), (1, 2), (3,), (4,))
    coarse_gots = [
        {(0, 0): jnp.concatenate([shares[at] for at in ranges], axis=0)}
        for ranges in coarse_ranges
    ]
    feed_gots = fine_gots + coarse_gots
    near_or_own = [o for o in offsets if not o[0]]

    def fetch_fine(index, chosen):
        if units[index]:
            fetch(fine_gots[index], chosen)

    def fetch_near(index):
        if coarse_gots[index][0, 0].shape[0]:
            fetch(coarse_gots[index], near_offsets)

    half_tokens, other_tokens, grad_kept = settle(half_tokens, other_tokens, grad_kept)
    both_tokens = [half_tokens, other_tokens]

    fetch(gate_got, near_offsets)
    fetch(out_got, near_offsets)
    fetch(out_got, far_offsets)
    key_here = count * key_part
    mix_wide = 2 * key_here + count * value_part
    mix_places = []
    for at in range(count):
        mix_places += [
            (at, 0, key_part, at * key_part),
            (at, key_part, key_part, key_here + at * key_part),
            (count + at, 0, value_part, 2 * key_here + at * value_part),
        ]
    mix_places.append((2 * count, 0, BETA_LANES, mix_wide))
    mix_given = [got[offset] for got in (head_got, value_got) for offset in offsets] + [beta_block]
    taps_all = [
        value_got[offset][value_part : value_part + KERNEL, :taps_wide] for offset in offsets
    ]
    taps = jnp.concatenate(
        [piece[:, :key_part] for piece in taps_all]
        + [piece[:, key_part : 2 * key_part] for piece in taps_all]
        + [piece[:, 2 * key_part :] for piece in taps_all],
        axis=1,
    ).astype(F32)
    taps = jnp.pad(taps, ((0, 8 - KERNEL), (0, 0)))
    feed_here = count * feed_part
    mix_rows, pre, beta_pre = run_project(
        both_tokens, mix_given, mix_places, gain_f[None], scale_all, mix_wide + BETA_LANES, mix_wide
    )
    groups[:] = [gate_got, out_got] + feed_gots
    both_tokens, pre, beta_pre, taps, grad_kept = settle(
        both_tokens, pre, beta_pre, taps, grad_kept
    )

    fetch(gate_got, cross_offsets)
    fetch(out_got, cross_offsets)
    fetch_fine(0, far_offsets)
    grad_x = along_x(grad_kept)
    grad_team = swap(grad_kept, "team", 1)
    pre = pre.reshape(outer + (rows, -1))
    beta_pre = beta_pre.reshape(outer + (rows, -1))
    place = jnp.full((1,), seq_pos, jnp.int32)
    head_outs, fresh, starts, solved = run_forward(place, pre, beta_pre, cols, rows_g, taps)
    groups[:] = [gate_got, out_got] + feed_gots
    both_tokens, head_outs, grad_x, grad_team = settle(both_tokens, head_outs, grad_x, grad_team)

    grad_half_rows = rows // 32 * 16

    def part_rows(pieces, start, stop):
        return [piece[start:stop] for piece in pieces]

    fetch_fine(0, cross_offsets)
    fetch_fine(1, far_offsets)
    grad_team_low = along_x(grad_team[:grad_half_rows])
    gate_wide = count * value_part
    head_outs = head_outs.reshape(2 * length, -1)
    gate_rows, out_rows, gate_other, mixed_other, branch_other = run_branch(
        1,
        both_tokens[1],
        [got[offset] for got in (gate_got, out_got) for offset in offsets],
        [(at, 0, value_part, at * value_part) for at in range(count)],
        [(count + at, 0, value_part, at * value_part) for at in range(count)],
        gain_f[None],
        scale_all,
        head_outs,
        gain_row,
    )
    groups[:] = feed_gots
    (
        both_tokens,
        grad_team,
        grad_team_low,
        gate_rows,
        out_rows,
        gate_other,
        mixed_other,
        branch_other,
    ) = settle(
        both_tokens,
        grad_team,
        grad_team_low,
        gate_rows,
        out_rows,
        gate_other,
        mixed_other,
        branch_other,
    )
    fetch_fine(1, cross_offsets)
    fetch_near(0)
    fetch_fine(2, far_offsets)
    grad_team_high = along_x(grad_team[grad_half_rows:])
    came_all = swap(branch_other, "seq", 1)
    whole = [(0, 0, gate_wide, 0)]
    _, _, gate_own, mixed_own, branch_own = run_branch(
        0,
        both_tokens[0],
        [gate_rows, out_rows],
        whole,
        [(1, 0, gate_wide, 0)],
        jnp.ones_like(gain_f)[None],
        scale_all,
        head_outs,
        gain_row,
    )
    came_all, grad_team_high, gate_own, mixed_own, branch_own = settle(
        came_all, grad_team_high, gate_own, mixed_own, branch_own
    )
    theirs, mine = fold_came(branch_own, came_all)
    grad_team_x = [
        jnp.concatenate([low, high], axis=0) for low, high in zip(grad_team_low, grad_team_high)
    ]
    fetch_fine(2, cross_offsets)
    fetch_near(1)
    fetch_fine(3, far_offsets)
    came = send_along(theirs)
    normed = run_norm(*after(tuple(both_tokens), *theirs.values()), scale_all, gain_f[None])
    theirs, mine, came, normed = settle(theirs, mine, came, normed)

    theirs = add_along(theirs, came)
    came = send_along(mine)
    came_team = swap(theirs, "team", 1)
    fetch_fine(3, cross_offsets)
    fetch_near(2)
    fetch_fine(4, far_offsets)
    grad_half = jnp.concatenate(list(grad_x) + list(grad_team_x), axis=0)
    mine, came, came_team, grad_half = settle(mine, came, came_team, grad_half)
    middle = source_f + add_along(mine, came).astype(F32) + came_team.astype(F32)

    feed_in = rms_scale(middle, feed_gain_f).astype(BF16)
    feed_x = along_x(feed_in)
    feed_team = swap(feed_in, "team", 1)
    fetch_fine(4, cross_offsets)
    fetch_near(3)
    grad_other = swap(grad_half, "seq", 1)
    all_rows = jnp.concatenate([mix_rows, gate_rows], axis=0)
    feed_x, feed_team, grad_half, grad_other, all_rows = settle(
        feed_x, feed_team, grad_half, grad_other, all_rows
    )
    seq_grads = [grad_half, grad_other]

    feed_team_x = along_x(feed_team)

    feed_places, down_places, feed_given = [], [], []
    for at, offset in enumerate(offsets):
        if offset[0]:
            spots = [(fine_gots[index][offset], 0, index) for index in range(len(units))]
        else:
            spots = []
            for got, ranges in zip(coarse_gots, coarse_ranges):
                start = 0
                for index in ranges:
                    spots.append((got.get(offset), start, index))
                    start += 3 * units[index]
        for piece, start, index in spots:
            size = units[index]
            if not size:
                continue
            which = next((n for n, given in enumerate(feed_given) if given is piece), None)
            if which is None:
                which = len(feed_given)
                feed_given.append(piece)
            target = starts_at[index] * count + at * size
            for kind in range(3):
                one = (which, start + kind * size, size)
                if kind < 2:
                    feed_places.append((*one, kind * feed_here + target))
                else:
                    down_places.append((*one, target))
    feed_rows, down_rows, *d_hiddens = run_hidden(
        seq_grads, feed_given, feed_places, down_places, feed_here
    )
    feed_half = jnp.concatenate(list(feed_x) + list(feed_team_x), axis=0)
    groups[:] = []
    feed_half, feed_rows, down_rows, d_hiddens = settle(feed_half, feed_rows, down_rows, d_hiddens)

    seq_feed = [feed_half, swap(feed_half, "seq", 1)]
    hidden_own, d_both_own, feed_own = run_feed(seq_feed[0], feed_rows, d_hiddens[0])
    hidden_other, d_both_other, feed_other = run_feed(seq_feed[1], feed_rows, d_hiddens[1])
    hiddens, d_boths = [hidden_own, hidden_other], [d_both_own, d_both_other]
    theirs, mine = fold_rows(feed_own, feed_other)
    kept = after((tuple(hiddens), tuple(d_boths)), *theirs.values())
    came = send_along(theirs)
    feed_low = run_outer(kept[1], seq_feed)
    theirs, mine, came, feed_low, hiddens = settle(theirs, mine, came, feed_low, list(kept[0]))

    theirs = add_along(theirs, came)
    came = send_along(mine)
    came_team = swap(theirs, "team", 1)
    down_low = run_outer(hiddens, seq_grads)
    rest = slice(3, None)

    def feed_pack(at, chosen):
        rows_of = []
        for values, base in ((feed_low, 0), (feed_low, feed_here), (down_low, 0)):
            for size, start in list(zip(units, starts_at))[chosen]:
                begin = base + start * count + at * size
                rows_of.append(values[begin : begin + size])
        return jnp.concatenate(rows_of, axis=0)

    far_all = [o for o in offsets if o[0]]
    near_all = [o for o in offsets if not o[0]]
    first_sent = {
        o: feed_pack(at, slice(0, 3)) for at, o in enumerate(offsets) if all(o)
    }
    mine, came, came_team, first_sent, feed_low, down_low = settle(
        mine, came, came_team, first_sent, feed_low, down_low
    )
    d_feed_in = add_along(mine, came).astype(F32) + came_team.astype(F32)

    feed_pull = jax.vjp(rms_scale, middle, feed_gain_f)[1]
    d_mid_norm, feed_gain_term = feed_pull(d_feed_in)
    d_middle = grad_own.astype(F32) + d_mid_norm
    d_branch = d_middle.astype(BF16)
    branch_x = along_x(d_branch)
    branch_team = swap(d_branch, "team", 1)
    first_came = send_bits(first_sent, "low", list(first_sent))
    first_pieces = {
        o: first_sent[o] if o in first_sent else feed_pack(at, slice(0, 3))
        for at, o in enumerate(offsets)
    }
    rest_pieces = {o: feed_pack(at, rest) for at, o in enumerate(offsets)}
    groups[:] = [first_pieces, rest_pieces]
    branch_x, branch_team, first_came, hiddens = settle(
        branch_x, branch_team, first_came, hiddens
    )

    branch_team_x = along_x(branch_team)
    first_pieces = add_bits(first_pieces, first_came)
    first_half = 3 * first_count // 2 // 16 * 16
    first_far = {
        o: swap(piece[:first_half], "high", o[0]) for o, piece in first_pieces.items() if o[0]
    }
    rest_came = send_bits(rest_pieces, "low", far_all)
    down_own, down_other = [product_tn(hidden, down_rows).astype(BF16) for hidden in hiddens]
    down_theirs, down_mine = fold_rows(down_own, down_other)
    branch_half = jnp.concatenate(list(branch_x) + list(branch_team_x), axis=0)
    groups[:] = [first_pieces, rest_pieces]
    branch_half, rest_came, down_theirs, down_mine, first_far = settle(
        branch_half, rest_came, down_theirs, down_mine, first_far
    )

    down_came = send_along(down_theirs)
    next_far = {
        o: swap(piece[first_half:], "high", o[0]) for o, piece in first_pieces.items() if o[0]
    }
    rest_near = send_bits(rest_pieces, "low", near_all)
    seq_branch = [branch_half, swap(branch_half, "seq", 1)]
    d_outs, d_gate_pre, head_gain_term, mixer_terms = run_mixer_back(
        seq_branch,
        out_rows,
        head_outs,
        [gate_own, gate_other],
        [mixed_own, mixed_other],
        normed,
        gain_row,
        value_part,
    )
    def gate_pack(at):
        return cut(mixer_terms, at, 2 * value_part)

    groups[:] = [rest_pieces, first_pieces]
    d_outs, down_theirs, down_mine, down_came, next_far, rest_near, mixer_terms = (
        settle(
            d_outs,
            down_theirs,
            down_mine,
            down_came,
            next_far,
            rest_near,
            mixer_terms,
        )
    )
    gate_first = {o: gate_pack(at) for at, o in enumerate(offsets) if all(o)}
    rest_pieces = add_bits(rest_pieces, rest_came)

    head_terms = head_gain_term[0].reshape(low_count, DV // low_count)
    head_terms = jnp.concatenate(
        [
            lax.dynamic_index_in_dim(head_terms, at ^ low_pos, 0, False)
            for at in range(low_count)
        ],
        axis=0,
    ).reshape(devices, head_part)
    head_terms = jnp.pad(head_terms, ((0, 0), (0, gain_part - head_part))).reshape(1, model)
    small_base = jnp.concatenate(
        [
            jnp.zeros((H + 1, model), F32),
            feed_gain_term[None],
            head_terms,
            jnp.zeros((5, model), F32),
        ],
        axis=0,
    )

    rest_far = send_bits(rest_pieces, "high", list(rest_pieces))
    gate_came = send_bits(gate_first, "low", list(gate_first))
    first_near = send_bits(first_pieces, "low", near_all)
    down_theirs = add_along(down_theirs, down_came)
    down_came = send_along(down_mine)
    down_team = swap(down_theirs, "team", 1)
    wide_shape = outer + (rows, -1)
    d_all, d_taps = run_backward(
        place,
        pre,
        d_outs.reshape(wide_shape),
        d_gate_pre.reshape(wide_shape),
        beta_pre,
        cols,
        rows_g,
        taps,
        fresh,
        starts,
        solved,
    )
    groups[:] = []
    small_base, mixer_terms, d_all, d_taps, down_mine, down_came, down_team, gate_came, rest_far, first_near = settle(
        small_base, mixer_terms, d_all, d_taps, down_mine, down_came, down_team, gate_came, rest_far, first_near
    )
    d_all = d_all.reshape(2 * length, -1)

    gate_later = {o: gate_pack(at) for at, o in enumerate(offsets) if not all(o)}
    gate_near = send_bits(gate_later, "low", near_all)
    gate_pieces = add_bits({**gate_first, **gate_later}, gate_came)
    gate_far = {
        o: swap(piece[:value_part], "high", o[0]) for o, piece in gate_pieces.items() if o[0]
    }
    d_all = after(d_all, *[piece for o, piece in gate_pieces.items() if o[0]])
    def taps_of(start, part):
        return d_taps[:KERNEL, start : start + count * part].reshape(KERNEL, count, part)

    taps_rows = jnp.concatenate(
        [
            taps_of(0, key_part),
            taps_of(key_here, key_part),
            taps_of(2 * key_here, value_part),
        ],
        axis=2,
    ).transpose(1, 0, 2)
    taps_rows = jnp.pad(taps_rows, ((0, 0), (0, 16 - KERNEL), (0, model - taps_wide)))
    taps_rows = taps_rows.reshape(count * 16, model).astype(BF16)
    mix_low = run_weigh(d_all, normed, taps_rows, (count, key_part, value_part))
    piece_rows = 2 * key_part + value_part + 16
    beta_term = mix_low[count * piece_rows : count * piece_rows + heads].astype(F32)

    def mix_pack(at):
        return cut(mix_low, at, piece_rows)

    groups[:] = [gate_pieces]
    d_all, gate_far, gate_near, mix_low, d_taps, down_mine, down_came, down_team = settle(
        d_all, gate_far, gate_near, mix_low, d_taps, down_mine, down_came, down_team
    )
    mix_sent = {o: mix_pack(at) for at, o in enumerate(offsets) if all(o)}

    def part_of(pieces, start, stop):
        return {o: piece[start:stop] for o, piece in pieces.items()}

    out_pieces = {o: piece[value_part:] for o, piece in gate_pieces.items() if o[0]}
    out_half = value_part // 32 * 16
    mix_half = (2 * key_part + value_part + 16) // 32 * 16
    out_far = send_bits(part_of(out_pieces, 0, out_half), "high", list(out_pieces))
    mix_came = send_bits(part_of(mix_sent, 0, mix_half), "low", list(mix_sent))
    normed_other, gain_other = run_back(d_all, all_rows, normed, 1)
    d_all, normed_other, gain_other, out_far, mix_came, out_pieces, mix_sent = settle(
        d_all, normed_other, gain_other, out_far, mix_came, out_pieces, mix_sent
    )
    out_next = send_bits(part_of(out_pieces, out_half, None), "high", list(out_pieces))
    mix_next = send_bits(part_of(mix_sent, mix_half, None), "low", list(mix_sent))
    came_other = swap(normed_other, "seq", 1)
    normed_own, gain_own = run_back(d_all, all_rows, normed, 0)
    groups[:] = [gate_pieces, first_pieces, rest_pieces]
    (
        normed_own,
        gain_own,
        came_other,
        out_next,
        mix_next,
        gain_other,
        down_mine,
        down_came,
        down_team,
        beta_term,
        mix_low,
    ) = settle(
        normed_own,
        gain_own,
        came_other,
        out_next,
        mix_next,
        gain_other,
        down_mine,
        down_came,
        down_team,
        beta_term,
        mix_low,
    )
    mix_came = {o: jnp.concatenate([mix_came[o], mix_next[o]], axis=0) for o in mix_came}
    theirs, _ = fold_came(normed_own, came_other)
    mixer_gain_term = (gain_own[0] + gain_other[0]) / (gain_f * gain_f)
    row_ids = lax.broadcasted_iota(jnp.int32, (H + 8, model), 0)
    small_rows = jnp.where(row_ids == H, mixer_gain_term[None], small_base)
    for head in range(heads):
        small_rows = jnp.where(row_ids == head_places[head], beta_term[head][None], small_rows)
    blocks = model // (low_count * gain_part)
    small_terms = small_rows.reshape(H + 8, blocks, -1).transpose(1, 0, 2)
    small_terms = small_terms.reshape(pieces_x, 2, high_count, 2, H + 8, -1)
    groups[:] = []
    theirs_sent = {at: piece for at, piece in theirs.items() if at}
    theirs_sent, normed_own, came_other, small_terms, mix_came, mix_sent, mix_low = settle(
        theirs_sent, normed_own, came_other, small_terms, mix_came, mix_sent, mix_low
    )

    mix_pieces = {
        o: mix_sent[o] if o in mix_sent else mix_pack(at) for at, o in enumerate(offsets)
    }
    mix_pieces = add_bits(mix_pieces, mix_came)
    groups[:] = [mix_pieces, gate_pieces, first_pieces, rest_pieces]
    theirs, mine = fold_came(normed_own, came_other)
    theirs.update(theirs_sent)
    came = send_along(theirs)
    mix_far = {
        o: swap(piece[: 2 * key_part], "high", o[0]) for o, piece in mix_pieces.items() if o[0]
    }
    mix_near = send_bits(mix_pieces, "low", near_all)
    small_terms = sum_stage(small_terms, "team", 3)
    small_terms = sum_stage(small_terms, "seq", 1, (1,))
    small_terms = sum_stage(small_terms, "high", 2)
    theirs, mine, came, small_terms, mix_far, mix_near, first_near, rest_near, rest_far = settle(
        theirs, mine, came, small_terms, mix_far, mix_near, first_near, rest_near, rest_far
    )

    theirs = add_along(theirs, came)
    came_team = swap(theirs, "team", 1)
    small_terms = sum_stage(small_terms, "seq", 0, bits_of(seq_count)[1:])
    came = send_along({at: after(piece, small_terms) for at, piece in mine.items()})
    for bit in bits_of(low_count):
        small_terms = small_terms + swap(small_terms, "low", bit)
    value_far = {
        o: swap(piece[2 * key_part :], "high", o[0]) for o, piece in mix_pieces.items() if o[0]
    }
    given = []

    def known(piece):
        for at, other in enumerate(given):
            if other is piece:
                return at
        given.append(piece)
        return len(given) - 1

    def segment(size, start, pieces, parts=()):
        sources = [(known(piece), start) for piece in pieces]
        for begin, more in parts:
            sources += [(known(piece), start - begin) for piece in more]
        return size, sources

    def spans(start, size, cut_at):
        if start < cut_at < start + size:
            return [(start, cut_at - start), (cut_at, start + size - cut_at)]
        return [(start, size)]

    mix_all = [mix_pieces[0, 0], *mix_near.values()]
    gate_all = [gate_pieces[0, 0], *gate_near.values()]
    first_all = [first_pieces[0, 0], *first_near.values()]
    rest_all = [rest_pieces[0, 0], *rest_near.values(), *rest_far.values()]
    rest_count = feed_part - first_count
    outputs = [
        ([segment(key_part, 0, mix_all + list(mix_far.values()))], False),
        ([segment(key_part, key_part, mix_all + list(mix_far.values()))], False),
        ([segment(value_part, 0, gate_all + list(gate_far.values()))], True),
        (
            [
                segment(
                    size,
                    start,
                    gate_all,
                    [
                        (value_part, out_far.values())
                        if start < value_part + out_half
                        else (value_part + out_half, out_next.values())
                    ],
                )
                for start, size in spans(value_part, value_part, value_part + out_half)
            ],
            False,
        ),
    ]
    for kind in range(3):
        segments = [
            segment(
                size,
                start,
                first_all,
                [(0, first_far.values()) if start < first_half else (first_half, next_far.values())],
            )
            for start, size in spans(kind * first_count, first_count, first_half)
        ]
        segments.append(segment(rest_count, kind * rest_count, rest_all))
        outputs.append((segments, False))
    finished = run_finish(given, outputs)
    mine, came, came_team, value_far, small_terms, finished = settle(
        mine, came, came_team, value_far, small_terms, finished
    )
    small_rows = small_terms.reshape(H + 8, low_count, gain_part)
    small_rows = sum(
        jnp.where(low_pos == at, small_rows[:, at], 0.0) for at in range(low_count)
    )
    beta_sum = small_rows[:H].T
    d_source = add_along(mine, came).astype(F32) + came_team.astype(F32)
    unit = source_f * scale_own
    d_norm = scale_own * (d_source - unit * jnp.mean(unit * d_source, axis=-1, keepdims=True))
    tokens_grad = (d_middle + d_norm).astype(BF16)[None]
    block_out = middle + add_along(down_mine, down_came).astype(F32) + down_team.astype(F32)
    block_out = block_out.astype(BF16)[None]

    value_sum = sum(
        [piece[2 * key_part :].astype(F32) for piece in mix_near.values()],
        mix_pieces[0, 0][2 * key_part :].astype(F32),
    )
    value_sum = sum([piece.astype(F32) for piece in value_far.values()], value_sum)
    taps_sum = value_sum[value_part : value_part + KERNEL, :taps_wide]

    return (
        block_out,
        tokens_grad,
        small_rows[H],
        finished[0].T,
        finished[1].T,
        value_sum[:value_part].T,
        beta_sum,
        finished[2],
        taps_sum[:, :key_part],
        taps_sum[:, key_part : 2 * key_part],
        taps_sum[:, 2 * key_part :],
        small_rows[H + 2, :head_part],
        finished[3],
        small_rows[H + 1],
        finished[4].T,
        finished[5].T,
        finished[6],
    )


def solution(mesh):
    in_specs = (
        P(BATCH, "seq", None),
        P(BATCH, None, "seq"),
        P(BATCH, "seq", None),
        P(ALL),
        P(None, ALL),
        P(None, ALL),
        P(None, ALL),
        P(ALL, None),
        P(None, ALL),
        P(None, ALL),
        P(None, ALL),
        P(None, ALL),
        P(ALL),
        P(ALL, None),
        P(ALL),
        P(None, ALL),
        P(None, ALL),
        P(ALL, None),
    )
    out_specs = (
        P(BATCH, "seq", None),
        P(BATCH, "seq", None),
        P(ALL),
        P(None, ALL),
        P(None, ALL),
        P(None, ALL),
        P(ALL, None),
        P(None, ALL),
        P(None, ALL),
        P(None, ALL),
        P(None, ALL),
        P(ALL),
        P(ALL, None),
        P(ALL),
        P(None, ALL),
        P(None, ALL),
        P(ALL, None),
    )
    seq_count, batch_count = mesh.shape["seq"], mesh.shape["batch"]
    team = seq_count * batch_count // H
    split = mesh.devices.reshape(seq_count, batch_count // (2 * team), 2, team)
    mesh = Mesh(split, ("seq", "high", "team", "low"))
    return jax.shard_map(local, mesh=mesh, in_specs=in_specs, out_specs=out_specs, check_vma=False)
```

```python
import functools

import jax
import jax.numpy as jnp
from jax import lax
from jax.experimental import pallas as pl
from jax.experimental.pallas import tpu as pltpu
from jax.sharding import Mesh, PartitionSpec as P

H = 16
DK = 128
DV = 256
CHUNK = 128
KERNEL = 4
HALO = 16
BETA_LANES = 128
BATCH = ("high", "team", "low")
ALL = ("seq", "high", "team", "low")
EPS_NORM = 1e-05
EPS_UNIT = 1e-06
F32 = jnp.float32
BF16 = jnp.bfloat16
VMEM_PARAMS = pltpu.CompilerParams(
    dimension_semantics=("arbitrary",), vmem_limit_bytes=52 * 1024 * 1024
)


def mm(a, b):
    return jnp.dot(a.astype(BF16), b.astype(BF16), preferred_element_type=F32)


def mm_nt(a, b):
    return lax.dot_general(
        a.astype(BF16), b.astype(BF16), (((1,), (1,)), ((), ())), preferred_element_type=F32
    )


def mm_tn(a, b):
    return lax.dot_general(
        a.astype(BF16), b.astype(BF16), (((0,), (0,)), ((), ())), preferred_element_type=F32
    )


def split_pair(a):
    high = a.astype(BF16)
    return high, (a - high.astype(F32)).astype(BF16)


def mm_fine(a, b):
    a_high, a_low = split_pair(a)
    b_high, b_low = split_pair(b)
    left = jnp.concatenate([a_high, a_low], axis=1)
    right = jnp.concatenate(
        [
            jnp.concatenate([b_high, b_low], axis=1),
            jnp.concatenate([b_high, jnp.zeros_like(b_low)], axis=1),
        ],
        axis=0,
    )
    both = jnp.dot(left, right, preferred_element_type=F32)
    wide = b.shape[1]
    return both[:, :wide] + both[:, wide:]


def sigmoid(v):
    return 1.0 / (1.0 + jnp.exp(-v))


def conv_cols(ext, seq, start, width, taps, rows):
    total = None
    for tap in range(KERNEL):
        term = taps[tap : tap + 1, start : start + width] * ext[
            seq, pl.ds(8 - (KERNEL - 1) + tap, rows), start : start + width
        ]
        total = term if total is None else total + term
    return total


def lower_masks(rows):
    row = lax.broadcasted_iota(jnp.int32, (rows, rows), 0)
    col = lax.broadcasted_iota(jnp.int32, (rows, rows), 1)
    return row, col


def inverse_many(couplings, row, col):
    rows = row.shape[0]
    eye = (row == col).astype(F32)
    pair = (row // 2 == col // 2)
    out = [eye - jnp.where(pair, a, 0.0) for a in couplings]
    size = 2
    while size < rows:
        mask = (row // (2 * size) == col // (2 * size)) & (row // size != col // size)
        inner = [mm_fine(jnp.where(mask, a, 0.0), t) for a, t in zip(couplings, out)]
        out = [t - mm_fine(t, i) for t, i in zip(out, inner)]
        size *= 2
    return out


def forward_body(
    heads, place, pre, strengths, cols, rows_g, taps, outs, fresh, starts, solved, ext, state
):
    chunk = pl.program_id(0)
    count = pre.shape[3]
    key_all = heads * DK

    @pl.when(chunk == 0)
    def _():
        ext[:, 0:8, :] = jnp.zeros((2, 8, ext.shape[2]), F32)
        state[...] = jnp.zeros(state.shape, F32)

    row, col = lower_masks(count)
    streams = [(seq, head) for seq in range(2) for head in range(heads)]
    for seq in range(2):
        ext[seq, 8 : 8 + count, :] = pre[0, seq, 0].astype(F32)
    queries, keys, values, ratios, couplings = [], [], [], [], []
    for seq, head in streams:
        q = conv_cols(ext, seq, head * DK, DK, taps, count)
        q = q * sigmoid(q)
        q = q * lax.rsqrt(jnp.sum(q * q, axis=1, keepdims=True) + EPS_UNIT)
        k = conv_cols(ext, seq, key_all + head * DK, DK, taps, count)
        k = k * sigmoid(k)
        k = k * lax.rsqrt(jnp.sum(k * k, axis=1, keepdims=True) + EPS_UNIT)
        v = conv_cols(ext, seq, 2 * key_all + head * DV, DV, taps, count)
        v = v * sigmoid(v)
        queries.append(q.astype(BF16))
        keys.append(k.astype(BF16))
        values.append(v.astype(BF16))
        g_col = cols[0, seq, 0, :, 3 * head : 3 * head + 1]
        g_row = rows_g[0, seq, 0, 0, head : head + 1, :]
        ratio = jnp.where(row >= col, jnp.exp(jnp.minimum(g_col - g_row, 0.0)), 0.0)
        ratios.append(ratio)
        beta = sigmoid(strengths[0, seq, 0, :, head : head + 1])
        couplings.append(jnp.where(row > col, beta * ratio * mm_nt(keys[-1], keys[-1]), 0.0))
    for seq in range(2):
        ext[seq, 0:8, :] = ext[seq, count : count + 8, :]
    inverses = inverse_many(couplings, row, col)
    for at, (seq, head) in enumerate(streams):
        q, k, v, ratio = queries[at], keys[at], values[at], ratios[at]
        beta = sigmoid(strengths[0, seq, 0, :, head : head + 1])
        grown = cols[0, seq, 0, :, 3 * head + 1 : 3 * head + 2]
        fade = cols[0, seq, 0, :, 3 * head + 2 : 3 * head + 3]
        held = state[at]
        held_low = held.astype(BF16)
        starts[0, at] = held_low
        inverse = inverses[at].astype(BF16)
        solved[0, at] = inverse
        right = beta * (v.astype(F32) - grown * mm(k, held_low))
        news = mm(inverse, right).astype(BF16)
        scores = ratio * mm_nt(q, k)
        out = mm(scores, news) + grown * mm(q, held_low)
        last = jnp.exp(rows_g[0, seq, 0, 0, head : head + 1, count - 1 : count])
        state[at] = last * held + mm_tn(fade * k.astype(F32), news)
        place_v = slice(head * DV, head * DV + DV)
        fresh[0, seq, 0, :, place_v] = news
        outs[0, seq, 0, :, place_v] = out.astype(BF16)


def backward_body(
    heads,
    place,
    pre,
    halo,
    d_outs,
    d_gate,
    strengths,
    cols,
    rows_g,
    taps,
    fresh,
    starts,
    solved,
    d_all,
    d_taps,
    ext,
    d_ext,
    d_state,
):
    step = pl.program_id(0)
    chunk = pl.num_programs(0) - 1 - step
    count = pre.shape[3]
    key_all = heads * DK

    @pl.when(step == 0)
    def _():
        d_ext[:, count : count + 8, :] = jnp.zeros((2, 8, d_ext.shape[2]), F32)
        d_state[...] = jnp.zeros(d_state.shape, F32)
        d_taps[...] = jnp.zeros(d_taps.shape, F32)

    row, col = lower_masks(count)
    streams = [(seq, head) for seq in range(2) for head in range(heads)]
    keep = jnp.where(chunk > 0, 1.0, 0.0)
    for seq in range(2):
        ext[seq, 0:8, :] = keep * halo[0, seq, 0].astype(F32)[HALO - 8 : HALO, :]
        ext[seq, 8 : 8 + count, :] = pre[0, seq, 0].astype(F32)
    d_betas = []
    for at, (seq, head) in enumerate(streams):
        beta = sigmoid(strengths[0, seq, 0, :, head : head + 1])
        g_col = cols[0, seq, 0, :, 3 * head : 3 * head + 1]
        grown = cols[0, seq, 0, :, 3 * head + 1 : 3 * head + 2]
        fade = cols[0, seq, 0, :, 3 * head + 2 : 3 * head + 3]
        g_row = rows_g[0, seq, 0, 0, head : head + 1, :]
        last = jnp.exp(g_row[:, count - 1 : count])

        q_conv = conv_cols(ext, seq, head * DK, DK, taps, count)
        q_sig = sigmoid(q_conv)
        q_act = q_conv * q_sig
        q_scale = lax.rsqrt(jnp.sum(q_act * q_act, axis=1, keepdims=True) + EPS_UNIT)
        q_unit = q_act * q_scale
        k_conv = conv_cols(ext, seq, key_all + head * DK, DK, taps, count)
        k_sig = sigmoid(k_conv)
        k_act = k_conv * k_sig
        k_scale = lax.rsqrt(jnp.sum(k_act * k_act, axis=1, keepdims=True) + EPS_UNIT)
        k_unit = k_act * k_scale
        v_conv = conv_cols(ext, seq, 2 * key_all + head * DV, DV, taps, count)
        v_sig = sigmoid(v_conv)
        q, k = q_unit.astype(BF16), k_unit.astype(BF16)
        v = (v_conv * v_sig).astype(BF16).astype(F32)
        k_full = k.astype(F32)

        place_v = slice(head * DV, head * DV + DV)
        d_out = d_outs[0, seq, 0, :, place_v]
        news = fresh[0, seq, 0, :, place_v]
        held = starts[0, at]
        inverse = solved[0, at]
        d_held = d_state[at]
        d_held_low = d_held.astype(BF16)
        ratio = jnp.where(row >= col, jnp.exp(jnp.minimum(g_col - g_row, 0.0)), 0.0)
        scores = ratio * mm_nt(q, k)
        d_news = mm_tn(scores, d_out) + mm(fade * k_full, d_held_low)
        d_right = mm_tn(inverse, d_news)
        d_right_low = d_right.astype(BF16)
        d_couple = jnp.where(row > col, -ratio * mm_nt(d_right_low, news), 0.0)
        key_key = mm_nt(k, k)
        d_kk = beta * d_couple
        d_scores = ratio * mm_nt(d_out, news)
        out_held = mm_nt(d_out, held)
        right_held = mm_nt(d_right_low, held)
        news_held = mm_nt(news, d_held_low)
        d_q = mm(d_scores, k) + grown * out_held
        d_k = (
            mm_tn(d_scores, q)
            + mm(d_kk, k)
            + mm_tn(d_kk, k)
            + fade * news_held
            - (beta * grown) * right_held
        )
        d_v = beta * d_right
        d_betas.append(
            jnp.sum(d_right * v, axis=1, keepdims=True)
            - grown * jnp.sum(right_held * k_full, axis=1, keepdims=True)
            + jnp.sum(d_couple * key_key, axis=1, keepdims=True)
        )
        d_state[at] = (
            last * d_held
            + mm_tn(grown * q.astype(F32), d_out)
            - mm_tn((beta * grown) * k_full, d_right_low)
        )
        d_qa = q_scale * (d_q - q_unit * jnp.sum(q_unit * d_q, axis=1, keepdims=True))
        d_ka = k_scale * (d_k - k_unit * jnp.sum(k_unit * d_k, axis=1, keepdims=True))
        d_ext[seq, 0:count, head * DK : head * DK + DK] = d_qa * (
            q_sig * (1.0 + q_conv * (1.0 - q_sig))
        )
        d_ext[seq, 0:count, key_all + head * DK : key_all + head * DK + DK] = d_ka * (
            k_sig * (1.0 + k_conv * (1.0 - k_sig))
        )
        d_ext[
            seq, 0:count, 2 * key_all + head * DV : 2 * key_all + head * DV + DV
        ] = d_v * (v_sig * (1.0 + v_conv * (1.0 - v_sig)))
    for seq in range(2):
        lane = lax.broadcasted_iota(jnp.int32, (count, BETA_LANES), 1)
        d_beta = jnp.zeros((count, BETA_LANES), F32)
        for head in range(heads):
            beta = sigmoid(strengths[0, seq, 0, :, head : head + 1])
            d_beta = jnp.where(
                lane == head, d_betas[seq * heads + head] * beta * (1.0 - beta), d_beta
            )
        wide = ext.shape[2]
        d_all[0, seq, 0, :, wide : wide + BETA_LANES] = d_beta.astype(BF16)
        d_all[0, seq, 0, :, wide + BETA_LANES :] = d_gate[0, seq, 0]
        for start in range(0, wide, 128):
            span = slice(start, start + 128)
            total = None
            near = d_ext[seq, 0:count, span]
            for tap in range(KERNEL):
                term = taps[tap : tap + 1, span] * d_ext[seq, pl.ds(KERNEL - 1 - tap, count), span]
                total = term if total is None else total + term
                moved = ext[seq, pl.ds(8 - (KERNEL - 1) + tap, count), span]
                d_taps[tap : tap + 1, span] += jnp.sum(near * moved, axis=0, keepdims=True)
            d_all[0, seq, 0, :, span] = total.astype(BF16)
        d_ext[seq, count : count + 8, :] = d_ext[seq, 0:8, :]


def chunk_block(chunk, place, per_piece):
    piece = jnp.bitwise_xor(chunk // per_piece, place[0])
    return piece % 2, piece // 2, chunk % per_piece


def chunk_specs(turn, per_piece):
    def by_rows(width):
        def index(step, at):
            half, piece, within = chunk_block(turn(step), at, per_piece)
            return (half, 0, piece, within, 0)

        return pl.BlockSpec((1, 2, 1, CHUNK, width), index)

    def by_chunk(heads):
        def index(step, at):
            half, piece, within = chunk_block(turn(step), at, per_piece)
            return (half, 0, piece, within, 0, 0)

        return pl.BlockSpec((1, 2, 1, 1, heads, CHUNK), index)

    return by_rows, by_chunk


def run_forward(place, pre, strengths, cols, rows_g, taps):
    halves, _, pieces, piece_rows, wide = pre.shape
    heads = rows_g.shape[-2]
    per_piece = piece_rows // CHUNK
    chunks = halves * pieces * per_piece
    by_rows, by_chunk = chunk_specs(lambda step: step, per_piece)
    grid_spec = pltpu.PrefetchScalarGridSpec(
        num_scalar_prefetch=1,
        grid=(chunks,),
        in_specs=[
            by_rows(wide),
            by_rows(BETA_LANES),
            by_rows(3 * heads),
            by_chunk(heads),
            pl.BlockSpec((8, wide), lambda c, at: (0, 0)),
        ],
        out_specs=[
            by_rows(heads * DV),
            by_rows(heads * DV),
            pl.BlockSpec((1, 2 * heads, DK, DV), lambda c, at: (c, 0, 0, 0)),
            pl.BlockSpec((1, 2 * heads, CHUNK, CHUNK), lambda c, at: (c, 0, 0, 0)),
        ],
        scratch_shapes=[
            pltpu.VMEM((2, CHUNK + 8, wide), F32),
            pltpu.VMEM((2 * heads, DK, DV), F32),
        ],
    )
    rows_out = jax.ShapeDtypeStruct(pre.shape[:-1] + (heads * DV,), BF16)
    return pl.pallas_call(
        functools.partial(forward_body, heads),
        grid_spec=grid_spec,
        out_shape=[
            rows_out,
            rows_out,
            jax.ShapeDtypeStruct((chunks, 2 * heads, DK, DV), BF16),
            jax.ShapeDtypeStruct((chunks, 2 * heads, CHUNK, CHUNK), BF16),
        ],
        compiler_params=VMEM_PARAMS,
        name="delta_forward",
    )(place, pre, strengths, cols, rows_g, taps)


def run_backward(
    place, pre, d_outs, d_gate, strengths, cols, rows_g, taps, fresh, starts, solved
):
    halves, _, pieces, piece_rows, wide = pre.shape
    heads = d_outs.shape[-1] // DV
    per_piece = piece_rows // CHUNK
    chunks = halves * pieces * per_piece
    per_halo = CHUNK // HALO
    wide_out = wide + BETA_LANES + heads * DV

    def turned(step):
        return chunks - 1 - step

    by_rows, by_chunk = chunk_specs(turned, per_piece)

    def halo_place(step, at):
        half, piece, within = chunk_block(jnp.maximum(turned(step) - 1, 0), at, per_piece)
        return (half, 0, piece, within * per_halo + per_halo - 1, 0)

    grid_spec = pltpu.PrefetchScalarGridSpec(
        num_scalar_prefetch=1,
        grid=(chunks,),
        in_specs=[
            by_rows(wide),
            pl.BlockSpec((1, 2, 1, HALO, wide), halo_place),
            by_rows(heads * DV),
            by_rows(heads * DV),
            by_rows(BETA_LANES),
            by_rows(3 * heads),
            by_chunk(heads),
            pl.BlockSpec((8, wide), lambda c, at: (0, 0)),
            by_rows(heads * DV),
            pl.BlockSpec((1, 2 * heads, DK, DV), lambda c, at: (turned(c), 0, 0, 0)),
            pl.BlockSpec((1, 2 * heads, CHUNK, CHUNK), lambda c, at: (turned(c), 0, 0, 0)),
        ],
        out_specs=[by_rows(wide_out), pl.BlockSpec((8, wide), lambda c, at: (0, 0))],
        scratch_shapes=[
            pltpu.VMEM((2, CHUNK + 8, wide), F32),
            pltpu.VMEM((2, CHUNK + 8, wide), F32),
            pltpu.VMEM((2 * heads, DK, DV), F32),
        ],
    )
    return pl.pallas_call(
        functools.partial(backward_body, heads),
        grid_spec=grid_spec,
        out_shape=[
            jax.ShapeDtypeStruct(pre.shape[:-1] + (wide_out,), BF16),
            jax.ShapeDtypeStruct((8, wide), F32),
        ],
        compiler_params=VMEM_PARAMS,
        name="delta_backward",
    )(place, pre, pre, d_outs, d_gate, strengths, cols, rows_g, taps, fresh, starts, solved)


def norm_body(half, other, scale, gain, out):
    step = pl.program_id(0)

    @pl.when(step < pl.num_programs(0) // 2)
    def _():
        out[...] = (half[...].astype(F32) * scale[...] * gain[...]).astype(BF16)

    @pl.when(step >= pl.num_programs(0) // 2)
    def _():
        out[...] = (other[...].astype(F32) * scale[...] * gain[...]).astype(BF16)


def run_norm(half, other, scale, gain):
    length, model = half.shape
    tile = 256
    steps = length // tile
    return pl.pallas_call(
        norm_body,
        grid=(2 * steps,),
        in_specs=[
            pl.BlockSpec((tile, model), lambda i: (jnp.minimum(i, steps - 1), 0)),
            pl.BlockSpec((tile, model), lambda i: (jnp.maximum(i - steps, 0), 0)),
            pl.BlockSpec((tile, 1), lambda i: (i, 0)),
            pl.BlockSpec((1, model), lambda i: (0, 0)),
        ],
        out_specs=pl.BlockSpec((tile, model), lambda i: (i, 0)),
        out_shape=jax.ShapeDtypeStruct((2 * length, model), BF16),
        compiler_params=VMEM_PARAMS,
        name="norm_rows",
    )(half, other, scale, gain)


def place_rows(pieces, places, out, gain=None):
    for piece, start, size, target in places:
        rows = pieces[piece][start : start + size, :]
        if gain is not None:
            rows = (rows.astype(F32) * gain[...]).astype(BF16)
        out[target : target + size, :] = rows


def project_body(count, places, narrow, half, other, gain, scale, *refs):
    pieces, weights, outs = refs[:count], refs[count], refs[count + 1 :]
    step, steps = pl.program_id(0), pl.num_programs(0) // 2

    @pl.when(step == 0)
    def _():
        place_rows(pieces, places, weights, gain)

    for chosen, tokens in ((step < steps, half), (step >= steps, other)):

        @pl.when(chosen)
        def _():
            sums = mm_nt(tokens[...], weights[...]) * scale[...]
            outs[0][...] = sums[:, :narrow].astype(BF16)
            if len(outs) > 1:
                outs[1][...] = sums[:, narrow:]


def whole_block(shape):
    return pl.BlockSpec(shape, lambda i: (0, 0), pipeline_mode=pl.Buffered(1))


def run_project(halves, pieces, places, gain, scale, wide, narrow):
    length, model = halves[0].shape
    tile = 256
    steps = length // tile
    out_shape = [jax.ShapeDtypeStruct((wide, model), BF16)]
    out_shape.append(jax.ShapeDtypeStruct((2 * length, narrow), BF16))
    if wide > narrow:
        out_shape.append(jax.ShapeDtypeStruct((2 * length, wide - narrow), F32))
    return pl.pallas_call(
        functools.partial(project_body, len(pieces), places, narrow),
        grid=(2 * steps,),
        in_specs=[
            pl.BlockSpec((tile, model), lambda i: (jnp.minimum(i, steps - 1), 0)),
            pl.BlockSpec((tile, model), lambda i: (jnp.maximum(i - steps, 0), 0)),
            whole_block((1, model)),
            pl.BlockSpec((tile, 1), lambda i: (i, 0)),
        ]
        + [whole_block(piece.shape) for piece in pieces],
        out_specs=[pl.BlockSpec((wide, model), lambda i: (0, 0))]
        + [pl.BlockSpec((tile, one.shape[1]), lambda i: (i, 0)) for one in out_shape[1:]],
        out_shape=out_shape,
        compiler_params=VMEM_PARAMS,
        name="project_rows",
    )(*halves, gain, scale, *pieces)


def hidden_body(count, feed_places, down_places, first, second, *refs):
    pieces, (feed_rows, down_rows, back_first, back_second) = refs[:count], refs[count:]
    step, steps = pl.program_id(0), pl.num_programs(0) // 2

    @pl.when(step == 0)
    def _():
        place_rows(pieces, feed_places, feed_rows)
        place_rows(pieces, down_places, down_rows)

    for chosen, grads, back in (
        (step < steps, first, back_first),
        (step >= steps, second, back_second),
    ):

        @pl.when(chosen)
        def _():
            back[...] = mm_nt(down_rows[...], grads[...]).astype(BF16)


def run_hidden(grads, pieces, feed_places, down_places, units):
    length, model = grads[0].shape
    tile = 256
    steps = length // tile
    return pl.pallas_call(
        functools.partial(hidden_body, len(pieces), feed_places, down_places),
        grid=(2 * steps,),
        in_specs=[
            pl.BlockSpec((tile, model), lambda i: (jnp.minimum(i, steps - 1), 0)),
            pl.BlockSpec((tile, model), lambda i: (jnp.maximum(i - steps, 0), 0)),
        ]
        + [whole_block(piece.shape) for piece in pieces],
        out_specs=[
            pl.BlockSpec((2 * units, model), lambda i: (0, 0)),
            pl.BlockSpec((units, model), lambda i: (0, 0)),
            pl.BlockSpec((units, tile), lambda i: (0, jnp.minimum(i, steps - 1))),
            pl.BlockSpec((units, tile), lambda i: (0, jnp.maximum(i - steps, 0))),
        ],
        out_shape=[
            jax.ShapeDtypeStruct((2 * units, model), BF16),
            jax.ShapeDtypeStruct((units, model), BF16),
            jax.ShapeDtypeStruct((units, length), BF16),
            jax.ShapeDtypeStruct((units, length), BF16),
        ],
        compiler_params=VMEM_PARAMS,
        name="hidden_cotangents",
    )(*grads, *pieces)


def feed_body(feed, weights, back, hidden, d_both, d_feed):
    units = back.shape[0]
    rows = feed[...]
    gate = mm_nt(weights[:units, :], rows)
    up = mm_nt(weights[units:, :], rows)
    sig = sigmoid(gate)
    smooth = gate * sig
    d_hidden = back[...].astype(F32)
    hidden[...] = (smooth * up).astype(BF16)
    d_gate = (d_hidden * up * (sig * (1.0 + gate * (1.0 - sig)))).astype(BF16)
    d_up = (d_hidden * smooth).astype(BF16)
    d_both[:units, :] = d_gate
    d_both[units:, :] = d_up
    d_feed[...] = (
        mm_tn(d_gate, weights[:units, :]) + mm_tn(d_up, weights[units:, :])
    ).astype(BF16)


def run_feed(feed, weights, back):
    length, model = feed.shape
    units = back.shape[0]
    tile = 256
    return pl.pallas_call(
        feed_body,
        grid=(length // tile,),
        in_specs=[
            pl.BlockSpec((tile, model), lambda i: (i, 0)),
            pl.BlockSpec((2 * units, model), lambda i: (0, 0)),
            pl.BlockSpec((units, tile), lambda i: (0, i)),
        ],
        out_specs=[
            pl.BlockSpec((units, tile), lambda i: (0, i)),
            pl.BlockSpec((2 * units, tile), lambda i: (0, i)),
            pl.BlockSpec((tile, model), lambda i: (i, 0)),
        ],
        out_shape=[
            jax.ShapeDtypeStruct((units, length), BF16),
            jax.ShapeDtypeStruct((2 * units, length), BF16),
            jax.ShapeDtypeStruct((length, model), BF16),
        ],
        compiler_params=VMEM_PARAMS,
        name="feed_forward",
    )(feed, weights, back)


def outer_body(first, second, right_first, right_second, out):
    out[...] = (
        mm(first[...], right_first[...]) + mm(second[...], right_second[...])
    ).astype(BF16)


def run_outer(lefts, rights):
    wide, length = lefts[0].shape
    model = rights[0].shape[1]
    tile = 176 if wide % 176 == 0 else wide
    left = pl.BlockSpec((tile, length), lambda i: (i, 0))
    right = pl.BlockSpec((length, model), lambda i: (0, 0))
    return pl.pallas_call(
        outer_body,
        grid=(wide // tile,),
        in_specs=[left, left, right, right],
        out_specs=pl.BlockSpec((tile, model), lambda i: (i, 0)),
        out_shape=jax.ShapeDtypeStruct((wide, model), BF16),
        compiler_params=VMEM_PARAMS,
        name="outer_sums",
    )(*lefts, *rights)


def back_body(d_rows, weights, normed, out, gain):
    @pl.when(pl.program_id(0) == 0)
    def _():
        gain[...] = jnp.zeros(gain.shape, F32)

    sums = mm(d_rows[...], weights[...])
    out[...] = sums.astype(BF16)
    gain[0:1, :] += jnp.sum(sums * normed[...].astype(F32), axis=0, keepdims=True)


def run_back(d_rows, weights, normed, half):
    length, wide = d_rows.shape[0] // 2, d_rows.shape[1]
    model = weights.shape[1]
    tile = 256
    start = half * (length // tile)
    return pl.pallas_call(
        back_body,
        grid=(length // tile,),
        in_specs=[
            pl.BlockSpec((tile, wide), lambda i: (start + i, 0)),
            pl.BlockSpec((wide, model), lambda i: (0, 0)),
            pl.BlockSpec((tile, model), lambda i: (start + i, 0)),
        ],
        out_specs=[
            pl.BlockSpec((tile, model), lambda i: (i, 0)),
            pl.BlockSpec((8, model), lambda i: (0, 0)),
        ],
        out_shape=[
            jax.ShapeDtypeStruct((length, model), BF16),
            jax.ShapeDtypeStruct((8, model), F32),
        ],
        compiler_params=VMEM_PARAMS,
        name="back_rows",
    )(d_rows, weights, normed)


def weigh_body(parts, d_rows, normed, taps, out):
    count, key_part, value_part = parts
    step = pl.program_id(0)
    piece = 2 * key_part + value_part + 16
    sums = mm_tn(d_rows[...], normed[...]).astype(BF16)
    tile = sums.shape[0]
    key_steps = count * key_part // tile
    value_steps = count * value_part // tile

    def store(part, first_step, offset):
        for at in range(tile // part):
            target = (step - first_step) * (tile // part) + at
            start = pl.multiple_of(target * piece + offset, 16)
            out[pl.ds(start, part), :] = sums[at * part : (at + 1) * part, :]

    @pl.when(step < key_steps)
    def _():
        store(key_part, 0, 0)

    @pl.when((step >= key_steps) & (step < 2 * key_steps))
    def _():
        store(key_part, key_steps, key_part)

    @pl.when((step >= 2 * key_steps) & (step < 2 * key_steps + value_steps))
    def _():
        store(value_part, 2 * key_steps, 2 * key_part)

    @pl.when(step == 2 * key_steps + value_steps)
    def _():
        out[count * piece : count * piece + tile, :] = sums
        for at in range(count):
            start = at * piece + piece - 16
            out[start : start + 16, :] = taps[at * 16 : at * 16 + 16, :]


def run_weigh(d_rows, normed, taps, parts):
    count, key_part, value_part = parts
    length = d_rows.shape[0]
    model = normed.shape[1]
    tile = 128
    wide = count * (2 * key_part + value_part)
    rows = wide + 16 * count + tile
    return pl.pallas_call(
        functools.partial(weigh_body, parts),
        grid=(wide // tile + 1,),
        in_specs=[
            pl.BlockSpec((length, tile), lambda i: (0, i)),
            whole_block((length, model)),
            whole_block(taps.shape),
        ],
        out_specs=pl.BlockSpec((rows, model), lambda i: (0, 0)),
        out_shape=jax.ShapeDtypeStruct((rows, model), BF16),
        compiler_params=VMEM_PARAMS,
        name="weight_sums",
    )(d_rows, normed, taps)


def mixer_back_body(
    heads,
    part,
    branch_own,
    branch_other,
    out_rows,
    head_outs,
    gate_own,
    gate_other,
    mixed_own,
    mixed_other,
    normed,
    gain,
    d_outs,
    d_gate,
    d_gain,
    terms,
    out_sums,
    gate_sums,
):
    step, steps = pl.program_id(0), pl.num_programs(0) // 2

    @pl.when(step == 0)
    def _():
        d_gain[...] = jnp.zeros(d_gain.shape, F32)
        out_sums[...] = jnp.zeros(out_sums.shape, F32)
        gate_sums[...] = jnp.zeros(gate_sums.shape, F32)

    for chosen, branch, gate, mixed in (
        (step < steps, branch_own, gate_own, mixed_own),
        (step >= steps, branch_other, gate_other, mixed_other),
    ):

        @pl.when(chosen)
        def _():
            d_mixed = mm_nt(branch[...], out_rows[...])
            out_sums[...] += mm_tn(mixed[...], branch[...])
            total = None
            for head in range(heads):
                span = slice(head * DV, head * DV + DV)
                out = head_outs[:, span].astype(F32)
                grad = d_mixed[:, span]
                g = gate[:, span].astype(F32)
                sig = sigmoid(g)
                scale = lax.rsqrt(jnp.mean(out * out, axis=1, keepdims=True) + EPS_NORM)
                unit = out * scale
                cot = grad * (g * sig)
                term = jnp.sum(cot * unit, axis=0, keepdims=True)
                total = term if total is None else total + term
                scaled = cot * gain[0:1, :]
                d_outs[:, span] = (
                    scale * (scaled - unit * jnp.mean(unit * scaled, axis=1, keepdims=True))
                ).astype(BF16)
                d_gate[:, span] = (
                    grad * unit * gain[0:1, :] * (sig * (1.0 + g * (1.0 - sig)))
                ).astype(BF16)
            d_gain[0:1, :] += total
            gate_sums[...] += mm_tn(d_gate[...], normed[...])

    @pl.when(step == 2 * steps - 1)
    def _():
        for at in range(out_sums.shape[0] // part):
            span = slice(at * part, (at + 1) * part)
            start = 2 * at * part
            terms[start : start + part, :] = gate_sums[span, :].astype(BF16)
            terms[start + part : start + 2 * part, :] = out_sums[span, :].astype(BF16)


def run_mixer_back(branches, out_rows, head_outs, gates, mixed, normed, gain, part):
    length, model = branches[0].shape
    wide = out_rows.shape[0]
    tile = 512
    steps = length // tile
    rows = pl.BlockSpec((tile, wide), lambda i: (i, 0))
    first = pl.BlockSpec((tile, wide), lambda i: (jnp.minimum(i, steps - 1), 0))
    second = pl.BlockSpec((tile, wide), lambda i: (jnp.maximum(i - steps, 0), 0))
    sums = pl.BlockSpec((2 * wide, model), lambda i: (0, 0))
    return pl.pallas_call(
        functools.partial(mixer_back_body, wide // DV, part),
        grid=(2 * steps,),
        in_specs=[
            pl.BlockSpec((tile, model), lambda i: (jnp.minimum(i, steps - 1), 0)),
            pl.BlockSpec((tile, model), lambda i: (jnp.maximum(i - steps, 0), 0)),
            whole_block((wide, model)),
            rows,
            first,
            second,
            first,
            second,
            pl.BlockSpec((tile, model), lambda i: (i, 0)),
            pl.BlockSpec((1, DV), lambda i: (0, 0)),
        ],
        out_specs=[rows, rows, pl.BlockSpec((8, DV), lambda i: (0, 0)), sums],
        out_shape=[
            jax.ShapeDtypeStruct((2 * length, wide), BF16),
            jax.ShapeDtypeStruct((2 * length, wide), BF16),
            jax.ShapeDtypeStruct((8, DV), F32),
            jax.ShapeDtypeStruct((2 * wide, model), BF16),
        ],
        scratch_shapes=[pltpu.VMEM((wide, model), F32), pltpu.VMEM((wide, model), F32)],
        compiler_params=VMEM_PARAMS,
        name="mixer_backward",
    )(*branches, out_rows, head_outs, *gates, *mixed, normed, gain)


def branch_body(count, gate_places, out_places, heads, tokens, gain, scale, head_outs, head_gain, *refs):
    pieces, (gate_rows, out_rows, gate, mixed, branch) = refs[:count], refs[count:]

    @pl.when(pl.program_id(0) == 0)
    def _():
        place_rows(pieces, gate_places, gate_rows, gain)
        place_rows(pieces, out_places, out_rows)

    gate_pre = mm_nt(tokens[...], gate_rows[...]) * scale[...]
    gate[...] = gate_pre.astype(BF16)
    for head in range(heads):
        span = slice(head * DV, head * DV + DV)
        out = head_outs[:, span].astype(F32)
        factor = lax.rsqrt(jnp.mean(out * out, axis=1, keepdims=True) + EPS_NORM)
        g = gate_pre[:, span]
        mixed[:, span] = (out * factor * head_gain[0:1, :] * (g * sigmoid(g))).astype(BF16)
    branch[...] = mm(mixed[...], out_rows[...]).astype(BF16)


def run_branch(half, tokens, pieces, gate_places, out_places, gain, scale, head_outs, head_gain):
    length, model = tokens.shape
    wide = head_outs.shape[1]
    tile = 256
    start = half * (length // tile)
    rows = pl.BlockSpec((tile, wide), lambda i: (i, 0))
    weights = pl.BlockSpec((wide, model), lambda i: (0, 0))
    return pl.pallas_call(
        functools.partial(branch_body, len(pieces), gate_places, out_places, wide // DV),
        grid=(length // tile,),
        in_specs=[
            pl.BlockSpec((tile, model), lambda i: (i, 0)),
            whole_block((1, model)),
            pl.BlockSpec((tile, 1), lambda i: (start + i, 0)),
            pl.BlockSpec((tile, wide), lambda i: (start + i, 0)),
            pl.BlockSpec((1, DV), lambda i: (0, 0)),
        ]
        + [whole_block(piece.shape) for piece in pieces],
        out_specs=[
            weights,
            weights,
            rows,
            rows,
            pl.BlockSpec((tile, model), lambda i: (i, 0)),
        ],
        out_shape=[
            jax.ShapeDtypeStruct((wide, model), BF16),
            jax.ShapeDtypeStruct((wide, model), BF16),
            jax.ShapeDtypeStruct((length, wide), BF16),
            jax.ShapeDtypeStruct((length, wide), BF16),
            jax.ShapeDtypeStruct((length, model), BF16),
        ],
        compiler_params=VMEM_PARAMS,
        name="branch_rows",
    )(tokens, gain, scale, head_outs, head_gain, *pieces)


def finish_body(count, outputs, *refs):
    given, outs = refs[:count], refs[count:]
    for (segments, turned), out in zip(outputs, outs):
        slabs = []
        for size, sources in segments:
            total = None
            for which, start in sources:
                term = given[which][start : start + size, :].astype(F32)
                total = term if total is None else total + term
            slabs.append(total)
        slab = slabs[0] if len(slabs) == 1 else jnp.concatenate(slabs, axis=0)
        if turned:
            rows = slab.shape[0]
            spare = -rows % 128
            if spare:
                slab = jnp.concatenate([slab, jnp.zeros((spare, slab.shape[1]), F32)], axis=0)
            out[...] = slab.T[:, :rows]
        else:
            out[...] = slab


def run_finish(given, outputs):
    model = given[0].shape[1]
    tile = 256
    out_specs, out_shape = [], []
    for segments, turned in outputs:
        rows = sum(size for size, _ in segments)
        if turned:
            out_specs.append(pl.BlockSpec((tile, rows), lambda i: (i, 0)))
            out_shape.append(jax.ShapeDtypeStruct((model, rows), F32))
        else:
            out_specs.append(pl.BlockSpec((rows, tile), lambda i: (0, i)))
            out_shape.append(jax.ShapeDtypeStruct((rows, model), F32))
    return pl.pallas_call(
        functools.partial(finish_body, len(given), outputs),
        grid=(model // tile,),
        in_specs=[pl.BlockSpec((piece.shape[0], tile), lambda i: (0, i)) for piece in given],
        out_specs=out_specs,
        out_shape=out_shape,
        compiler_params=VMEM_PARAMS,
        name="finish_sums",
    )(*given)


def product(left_side, right_side):
    return jnp.dot(left_side, right_side, preferred_element_type=F32)


def product_tn(left_side, right_side):
    return lax.dot_general(
        left_side, right_side, (((0,), (0,)), ((), ())), preferred_element_type=F32
    )


def product_nt(left_side, right_side):
    return lax.dot_general(
        left_side, right_side, (((1,), (1,)), ((), ())), preferred_element_type=F32
    )


def rms_scale(values, gain_vals):
    return (
        values * lax.rsqrt(jnp.mean(values * values, axis=-1, keepdims=True) + EPS_NORM) * gain_vals
    )


def swap(values, axis, bit):
    count = lax.axis_size(axis)
    return lax.ppermute(values, axis, [(place, place ^ bit) for place in range(count)])


def bits_of(count):
    found = []
    bit = 1
    while bit < count:
        found.append(bit)
        bit *= 2
    return found


def after(values, *earlier):
    return lax.optimization_barrier((values, *earlier))[0]


def add_low(left_side, right_side):
    return (left_side.astype(F32) + right_side.astype(F32)).astype(BF16)


def along_x(first):
    count = lax.axis_size("seq") // 2
    pieces = {0: first}
    for offset in sorted(range(1, count), key=lambda o: (-(o & -o), o)):
        low = offset & -offset
        pieces[offset] = swap(pieces[offset ^ low], "seq", 2 * low)
    return [pieces[offset] for offset in range(count)]


def fold_rows(part_own, part_other):
    return fold_came(part_own, swap(part_other, "seq", 1))


def fold_came(part_own, came):
    count = lax.axis_size("seq") // 2
    rows = part_own.shape[0] // (2 * count)
    folded = []
    for start in (count, 0):
        pieces = {}
        for at in reversed(range(count)):
            span = slice((start + at) * rows, (start + at + 1) * rows)
            pieces[at] = add_low(part_own[span], came[span])
        folded.append(pieces)
    return folded


def fold_first(part_own, came):
    theirs = fold_came(part_own, came)[0]
    sent = {at: piece for at, piece in theirs.items() if at}
    part_own, came, sent = lax.optimization_barrier((part_own, came, sent))
    theirs, mine = fold_came(part_own, came)
    theirs.update(sent)
    return theirs, mine


def send_along(pieces):
    return {at: swap(piece, "seq", 2 * at) for at, piece in pieces.items() if at}


def add_along(pieces, came):
    return sum(
        [piece.astype(F32) for piece in came.values()], pieces[0].astype(F32)
    ).astype(BF16)


def cut(values, at, size):
    return values[at * size : (at + 1) * size]


def send_bits(pieces, axis, chosen):
    at = 1 if axis == "low" else 0
    return {
        offset: swap(pieces[offset], axis, offset[at]) for offset in chosen if offset[at]
    }


def add_bits(pieces, came, hold=()):
    pieces = dict(pieces)
    for offset, piece in came.items():
        pieces.pop(offset)
        target = (offset[0], 0)
        kept = after(pieces[target], *hold) if hold else pieces[target]
        total = kept.astype(F32) + piece.astype(F32)
        pieces[target] = total if target == (0, 0) else total.astype(BF16)
    return pieces


def sum_pieces(pieces, near, far):
    return sum(
        [piece.astype(F32) for piece in (*near.values(), *far.values())],
        pieces[0, 0].astype(F32),
    )


def spread_stage(values, axis, bits=None):
    for bit in bits_of(lax.axis_size(axis)) if bits is None else bits:
        came = swap(values, axis, bit)
        values = jnp.where(
            (lax.axis_index(axis) & bit) == 0,
            jnp.concatenate([values, came], axis=0),
            jnp.concatenate([came, values], axis=0),
        )
    return values


def sum_stage(values, axis, dim, bits=None):
    for bit in reversed(bits_of(lax.axis_size(axis)) if bits is None else bits):
        lower, upper = jnp.split(values, 2, axis=dim)
        is_upper = (lax.axis_index(axis) & bit) != 0
        kept = jnp.where(is_upper, upper, lower)
        values = kept + swap(jnp.where(is_upper, lower, upper), axis, bit)
    return values


def local(
    tokens,
    decays,
    out_grad,
    mixer_gain,
    query_weight,
    key_weight,
    value_weight,
    beta_weight,
    outgate_weight,
    query_conv,
    key_conv,
    value_conv,
    head_gain,
    output_weight,
    feed_gain,
    feed_gate,
    feed_up,
    feed_down,
):
    seq_count = lax.axis_size("seq")
    high_count = lax.axis_size("high")
    low_count = lax.axis_size("low")
    seq_pos = lax.axis_index("seq")
    low_pos = lax.axis_index("low")
    devices = seq_count * high_count * 2 * low_count
    heads = high_count
    source = tokens[0]
    grad_own = out_grad[0]
    rows, model = source.shape
    length = rows * seq_count
    pieces_x = seq_count // 2
    key_part = query_weight.shape[1]
    value_part = value_weight.shape[1]
    feed_part = feed_gate.shape[1]
    gain_part = mixer_gain.shape[0]
    head_part = head_gain.shape[0]
    offsets = [(high, low) for high in range(high_count) for low in range(low_count)]
    count = len(offsets)
    far_offsets = [o for o in offsets if o[0] and not o[1]]
    near_offsets = [o for o in offsets if not o[0] and o[1]]
    cross_offsets = [o for o in offsets if o[0] and o[1]]

    groups = []

    def settle(*values):
        places = [(got, offset) for got in groups for offset in got]
        values, pieces = lax.optimization_barrier(
            (values, [got[offset] for got, offset in places])
        )
        for (got, offset), piece in zip(places, pieces):
            got[offset] = piece
        return values

    def fetch(got, chosen):
        if not got[0, 0].shape[0]:
            return
        for high, low in sorted(chosen, key=lambda o: (o[0], -(o[1] & -o[1]), o[1])):
            if low == 0:
                axis, bit, start = "high", high & -high, (high ^ (high & -high), 0)
            else:
                axis, bit, start = "low", low & -low, (high, low ^ (low & -low))
            got[high, low] = swap(got[start], axis, bit)

    def joined(got, start, size):
        return [got[offset][start : start + size] for offset in offsets]

    source_f = source.astype(F32)
    scale_own = lax.rsqrt(jnp.mean(source_f * source_f, axis=-1, keepdims=True) + EPS_NORM)
    small = jnp.concatenate([mixer_gain, feed_gain, beta_weight.T.reshape(-1), head_gain], axis=0)
    small_size = small.shape[0]
    small = jnp.pad(small, (0, -small_size % 2048)).reshape(1, -1, 128)
    small = spread_stage(small, "high")
    small = spread_stage(small, "low")
    small = spread_stage(small, "team")
    logs = jnp.concatenate([jnp.log(decays[0]), scale_own.reshape(1, rows)], axis=0)
    logs = jnp.pad(logs, ((0, -logs.shape[0] % 8), (0, 0)))
    logs = jnp.stack([logs, swap(logs, "team", 1)], axis=0)[:, None]
    taps_own = jnp.concatenate([query_conv, key_conv, value_conv], axis=1)
    taps_wide = taps_own.shape[1]
    taps_rows = jnp.pad(taps_own, ((0, 16 - KERNEL), (0, model - taps_wide)))
    head_got = {(0, 0): jnp.concatenate([query_weight.T, key_weight.T], axis=0)}
    value_got = {(0, 0): jnp.concatenate([value_weight.T, taps_rows], axis=0)}
    groups += [head_got]
    source_x = along_x(source)
    small, logs, source_kept, grad_kept = settle(small, logs, source, grad_own)

    source_team = swap(source_kept, "team", 1)
    fetch(head_got, far_offsets)
    fetch(head_got, near_offsets)
    groups += [value_got]
    small = spread_stage(small, "seq", (1,))
    small = spread_stage(after(small, source_x[-1]), "seq", bits_of(seq_count)[1:])
    for bit in bits_of(seq_count)[1:]:
        logs = jnp.concatenate([logs, swap(after(logs, source_x[-1]), "seq", bit)], axis=1)
    logs = jnp.stack([logs, swap(logs, "seq", 1)], axis=0)
    small, logs, source_x, source_team = settle(small, logs, source_x, source_team)

    team_x = along_x(source_team)
    fetch(value_got, far_offsets)
    fetch(head_got, cross_offsets)
    fetch(value_got, near_offsets)
    gate_got = {(0, 0): outgate_weight.T}
    out_got = {(0, 0): output_weight}
    groups += [gate_got, out_got]
    small_all = small.reshape((seq_count, 2, low_count, high_count, -1)).transpose(0, 3, 1, 2, 4)
    small_all = small_all.reshape(devices, -1)
    gain_f = small_all[:, :gain_part].reshape(-1).astype(F32)
    feed_gain_f = small_all[:, gain_part : 2 * gain_part].reshape(-1).astype(F32)
    beta_rows = (
        small_all[:, 2 * gain_part : 2 * gain_part + H * gain_part]
        .reshape(devices, H, gain_part)
        .transpose(1, 0, 2)
        .reshape(H, model)
    )
    head_gain_all = small_all[:, small_size - head_part : small_size].reshape(-1)
    gain_blocks = head_gain_all.reshape(low_count, DV // low_count)
    gain_row = jnp.concatenate(
        [
            lax.dynamic_index_in_dim(gain_blocks, at ^ low_pos, 0, False)
            for at in range(low_count)
        ],
        axis=0,
    ).astype(F32)[None]
    head_places = [
        seq_pos * (2 * heads) + 2 * (lax.axis_index("high") ^ head) + lax.axis_index("team")
        for head in range(heads)
    ]
    beta_own = jnp.stack(
        [lax.dynamic_index_in_dim(beta_rows, place, 0, False) for place in head_places], axis=0
    )

    head_logs = jnp.stack(
        [lax.dynamic_index_in_dim(logs, place, 3, False) for place in head_places], axis=3
    )
    outer = (2, 2, pieces_x)
    scale_all = logs[:, :, :, H].reshape(2 * length, 1)
    per_piece = rows // CHUNK
    totals = jnp.cumsum(head_logs.reshape(outer + (heads, per_piece, CHUNK)), axis=-1)
    rows_g = totals.transpose(0, 1, 2, 4, 3, 5)

    def as_cols(values):
        return values.transpose(0, 1, 2, 4, 5, 3).reshape(outer + (rows, heads))

    totals_cols = as_cols(totals)
    fade_cols = as_cols(jnp.exp(totals[..., -1:] - totals))

    half_tokens = jnp.concatenate(list(source_x) + list(team_x), axis=0)
    (
        half_tokens,
        grad_kept,
        gain_f,
        feed_gain_f,
        beta_own,
        gain_row,
        scale_all,
        rows_g,
        cols,
        beta_block,
    ) = settle(
        half_tokens,
        grad_kept,
        gain_f,
        feed_gain_f,
        beta_own,
        gain_row,
        scale_all,
        rows_g,
        jnp.stack([totals_cols, jnp.exp(totals_cols), fade_cols], axis=-1).reshape(
            outer + (rows, 3 * heads)
        ),
        jnp.pad(beta_own, ((0, BETA_LANES - heads), (0, 0))),
    )

    other_tokens = swap(half_tokens, "seq", 1)
    fetch(value_got, cross_offsets)
    fetch(gate_got, far_offsets)

    ends = [feed_part * part // 11 // 16 * 16 for part in (4, 5, 6, 9)] + [feed_part]
    starts_at = [0] + ends[:-1]
    units = [end - start for start, end in zip(starts_at, ends)]
    first_count = ends[2]
    rest_count = feed_part - first_count
    shares = []
    for start, end in zip(starts_at, ends):
        span = slice(start, end)
        shares.append(
            jnp.concatenate([feed_gate[:, span].T, feed_up[:, span].T, feed_down[span]], axis=0)
        )
    fine_gots = [{(0, 0): share} for share in shares]
    coarse_ranges = ((0,), (1, 2), (3,), (4,))
    coarse_gots = [
        {(0, 0): jnp.concatenate([shares[at] for at in ranges], axis=0)}
        for ranges in coarse_ranges
    ]
    feed_gots = fine_gots + coarse_gots
    near_or_own = [o for o in offsets if not o[0]]

    def fetch_fine(index, chosen):
        if units[index]:
            fetch(fine_gots[index], chosen)

    def fetch_near(index):
        if coarse_gots[index][0, 0].shape[0]:
            fetch(coarse_gots[index], near_offsets)

    half_tokens, other_tokens, grad_kept = settle(half_tokens, other_tokens, grad_kept)
    both_tokens = [half_tokens, other_tokens]

    fetch(gate_got, near_offsets)
    fetch(out_got, near_offsets)
    fetch(out_got, far_offsets)
    key_here = count * key_part
    mix_wide = 2 * key_here + count * value_part
    mix_places = []
    for at in range(count):
        mix_places += [
            (at, 0, key_part, at * key_part),
            (at, key_part, key_part, key_here + at * key_part),
            (count + at, 0, value_part, 2 * key_here + at * value_part),
        ]
    mix_places.append((2 * count, 0, BETA_LANES, mix_wide))
    mix_given = [got[offset] for got in (head_got, value_got) for offset in offsets] + [beta_block]
    taps_all = [
        value_got[offset][value_part : value_part + KERNEL, :taps_wide] for offset in offsets
    ]
    taps = jnp.concatenate(
        [piece[:, :key_part] for piece in taps_all]
        + [piece[:, key_part : 2 * key_part] for piece in taps_all]
        + [piece[:, 2 * key_part :] for piece in taps_all],
        axis=1,
    ).astype(F32)
    taps = jnp.pad(taps, ((0, 8 - KERNEL), (0, 0)))
    feed_here = count * feed_part
    mix_rows, pre, beta_pre = run_project(
        both_tokens, mix_given, mix_places, gain_f[None], scale_all, mix_wide + BETA_LANES, mix_wide
    )
    groups[:] = [gate_got, out_got] + feed_gots
    both_tokens, pre, beta_pre, taps, grad_kept = settle(
        both_tokens, pre, beta_pre, taps, grad_kept
    )

    fetch(gate_got, cross_offsets)
    fetch(out_got, cross_offsets)
    fetch_fine(0, far_offsets)
    grad_x = along_x(grad_kept)
    grad_team = swap(grad_kept, "team", 1)
    pre = pre.reshape(outer + (rows, -1))
    beta_pre = beta_pre.reshape(outer + (rows, -1))
    place = jnp.full((1,), seq_pos, jnp.int32)
    head_outs, fresh, starts, solved = run_forward(place, pre, beta_pre, cols, rows_g, taps)
    groups[:] = [gate_got, out_got] + feed_gots
    both_tokens, head_outs, grad_x, grad_team = settle(both_tokens, head_outs, grad_x, grad_team)

    grad_half_rows = rows // 32 * 16

    def part_rows(pieces, start, stop):
        return [piece[start:stop] for piece in pieces]

    fetch_fine(0, cross_offsets)
    fetch_fine(1, far_offsets)
    grad_team_low = along_x(grad_team[:grad_half_rows])
    gate_wide = count * value_part
    head_outs = head_outs.reshape(2 * length, -1)
    gate_rows, out_rows, gate_other, mixed_other, branch_other = run_branch(
        1,
        both_tokens[1],
        [got[offset] for got in (gate_got, out_got) for offset in offsets],
        [(at, 0, value_part, at * value_part) for at in range(count)],
        [(count + at, 0, value_part, at * value_part) for at in range(count)],
        gain_f[None],
        scale_all,
        head_outs,
        gain_row,
    )
    groups[:] = feed_gots
    (
        both_tokens,
        grad_team,
        grad_team_low,
        gate_rows,
        out_rows,
        gate_other,
        mixed_other,
        branch_other,
    ) = settle(
        both_tokens,
        grad_team,
        grad_team_low,
        gate_rows,
        out_rows,
        gate_other,
        mixed_other,
        branch_other,
    )
    fetch_fine(1, cross_offsets)
    fetch_near(1)
    fetch_fine(2, far_offsets)
    grad_team_high = along_x(grad_team[grad_half_rows:])
    came_all = swap(branch_other, "seq", 1)
    whole = [(0, 0, gate_wide, 0)]
    _, _, gate_own, mixed_own, branch_own = run_branch(
        0,
        both_tokens[0],
        [gate_rows, out_rows],
        whole,
        [(1, 0, gate_wide, 0)],
        jnp.ones_like(gain_f)[None],
        scale_all,
        head_outs,
        gain_row,
    )
    came_all, grad_team_high, gate_own, mixed_own, branch_own = settle(
        came_all, grad_team_high, gate_own, mixed_own, branch_own
    )
    theirs, mine = fold_first(branch_own, came_all)
    grad_team_x = [
        jnp.concatenate([low, high], axis=0) for low, high in zip(grad_team_low, grad_team_high)
    ]
    fetch_fine(2, cross_offsets)
    fetch_near(0)
    fetch_fine(3, far_offsets)
    came = send_along(theirs)
    normed = run_norm(*after(tuple(both_tokens), *theirs.values()), scale_all, gain_f[None])
    theirs, mine, came, normed = settle(theirs, mine, came, normed)

    theirs = add_along(theirs, came)
    came = send_along(mine)
    came_team = swap(theirs, "team", 1)
    fetch_fine(3, cross_offsets)
    fetch_near(2)
    fetch_fine(4, far_offsets)
    grad_half = jnp.concatenate(list(grad_x) + list(grad_team_x), axis=0)
    mine, came, came_team, grad_half = settle(mine, came, came_team, grad_half)
    middle = source_f + add_along(mine, came).astype(F32) + came_team.astype(F32)

    feed_in = rms_scale(middle, feed_gain_f).astype(BF16)
    feed_x = along_x(feed_in)
    feed_team = swap(feed_in, "team", 1)
    fetch_fine(4, cross_offsets)
    fetch_near(3)
    grad_other = swap(grad_half, "seq", 1)
    all_rows = jnp.concatenate([mix_rows, gate_rows], axis=0)
    feed_x, feed_team, grad_half, grad_other, all_rows = settle(
        feed_x, feed_team, grad_half, grad_other, all_rows
    )
    seq_grads = [grad_half, grad_other]

    feed_team_x = along_x(feed_team)

    feed_places, down_places, feed_given = [], [], []
    for at, offset in enumerate(offsets):
        if offset[0]:
            spots = [(fine_gots[index][offset], 0, index) for index in range(len(units))]
        else:
            spots = []
            for got, ranges in zip(coarse_gots, coarse_ranges):
                start = 0
                for index in ranges:
                    spots.append((got.get(offset), start, index))
                    start += 3 * units[index]
        for piece, start, index in spots:
            size = units[index]
            if not size:
                continue
            which = next((n for n, given in enumerate(feed_given) if given is piece), None)
            if which is None:
                which = len(feed_given)
                feed_given.append(piece)
            set_start, set_count = (0, first_count) if index < 3 else (first_count, rest_count)
            target = set_start * count + at * set_count + starts_at[index] - set_start
            for kind in range(3):
                one = (which, start + kind * size, size)
                if kind < 2:
                    feed_places.append((*one, kind * feed_here + target))
                else:
                    down_places.append((*one, target))
    feed_rows, down_rows, *d_hiddens = run_hidden(
        seq_grads, feed_given, feed_places, down_places, feed_here
    )
    feed_half = jnp.concatenate(list(feed_x) + list(feed_team_x), axis=0)
    groups[:] = []
    feed_half, feed_rows, down_rows, d_hiddens = settle(feed_half, feed_rows, down_rows, d_hiddens)

    seq_feed = [feed_half, swap(feed_half, "seq", 1)]
    hidden_own, d_both_own, feed_own = run_feed(seq_feed[0], feed_rows, d_hiddens[0])
    hidden_other, d_both_other, feed_other = run_feed(seq_feed[1], feed_rows, d_hiddens[1])
    hiddens, d_boths = [hidden_own, hidden_other], [d_both_own, d_both_other]
    theirs, mine = fold_first(feed_own, swap(feed_other, "seq", 1))
    kept = after((tuple(hiddens), tuple(d_boths)), *theirs.values())
    came = send_along(theirs)
    feed_low = run_outer(kept[1], seq_feed)
    theirs, mine, came, feed_low, hiddens = settle(theirs, mine, came, feed_low, list(kept[0]))

    theirs = add_along(theirs, came)
    came = send_along(mine)
    came_team = swap(theirs, "team", 1)
    down_low = run_outer(hiddens, seq_grads)

    def feed_pack(at, start, size):
        begin = start * count + at * size
        return jnp.concatenate(
            [
                feed_low[begin : begin + size],
                feed_low[feed_here + begin : feed_here + begin + size],
                down_low[begin : begin + size],
            ],
            axis=0,
        )

    far_all = [o for o in offsets if o[0]]
    near_all = [o for o in offsets if not o[0]]
    first_sent = {
        o: feed_pack(at, 0, first_count) for at, o in enumerate(offsets) if all(o)
    }
    mine, came, came_team, first_sent, feed_low, down_low = settle(
        mine, came, came_team, first_sent, feed_low, down_low
    )
    d_feed_in = add_along(mine, came).astype(F32) + came_team.astype(F32)

    feed_pull = jax.vjp(rms_scale, middle, feed_gain_f)[1]
    d_mid_norm, feed_gain_term = feed_pull(d_feed_in)
    d_middle = grad_own.astype(F32) + d_mid_norm
    d_branch = d_middle.astype(BF16)
    branch_x = along_x(d_branch)
    branch_team = swap(d_branch, "team", 1)
    first_came = send_bits(first_sent, "low", list(first_sent))
    first_pieces = {
        o: first_sent[o] if o in first_sent else feed_pack(at, 0, first_count)
        for at, o in enumerate(offsets)
    }
    rest_pieces = {o: feed_pack(at, first_count, rest_count) for at, o in enumerate(offsets)}
    groups[:] = [first_pieces, rest_pieces]
    branch_x, branch_team, first_came, hiddens = settle(
        branch_x, branch_team, first_came, hiddens
    )

    branch_team_x = along_x(branch_team)
    first_pieces = add_bits(first_pieces, first_came)
    first_half = 3 * first_count // 2 // 16 * 16
    first_far = {
        o: swap(piece[:first_half], "high", o[0]) for o, piece in first_pieces.items() if o[0]
    }
    rest_came = send_bits(rest_pieces, "low", far_all)
    down_own, down_other = [product_tn(hidden, down_rows).astype(BF16) for hidden in hiddens]
    down_theirs, down_mine = fold_rows(down_own, down_other)
    branch_half = jnp.concatenate(list(branch_x) + list(branch_team_x), axis=0)
    groups[:] = [first_pieces, rest_pieces]
    branch_half, rest_came, down_theirs, down_mine, first_far = settle(
        branch_half, rest_came, down_theirs, down_mine, first_far
    )

    down_came = send_along(down_theirs)
    next_far = {
        o: swap(piece[first_half:], "high", o[0]) for o, piece in first_pieces.items() if o[0]
    }
    rest_near = send_bits(rest_pieces, "low", near_all)
    seq_branch = [branch_half, swap(branch_half, "seq", 1)]
    d_outs, d_gate_pre, head_gain_term, mixer_terms = run_mixer_back(
        seq_branch,
        out_rows,
        head_outs,
        [gate_own, gate_other],
        [mixed_own, mixed_other],
        normed,
        gain_row,
        value_part,
    )
    def gate_pack(at):
        return cut(mixer_terms, at, 2 * value_part)

    groups[:] = [rest_pieces, first_pieces]
    d_outs, down_theirs, down_mine, down_came, next_far, rest_near, mixer_terms = (
        settle(
            d_outs,
            down_theirs,
            down_mine,
            down_came,
            next_far,
            rest_near,
            mixer_terms,
        )
    )
    gate_first = {o: gate_pack(at) for at, o in enumerate(offsets) if all(o)}
    rest_pieces = add_bits(rest_pieces, rest_came)

    head_terms = head_gain_term[0].reshape(low_count, DV // low_count)
    head_terms = jnp.concatenate(
        [
            lax.dynamic_index_in_dim(head_terms, at ^ low_pos, 0, False)
            for at in range(low_count)
        ],
        axis=0,
    ).reshape(devices, head_part)
    head_terms = jnp.pad(head_terms, ((0, 0), (0, gain_part - head_part))).reshape(1, model)
    small_base = jnp.concatenate(
        [
            jnp.zeros((H + 1, model), F32),
            feed_gain_term[None],
            head_terms,
            jnp.zeros((5, model), F32),
        ],
        axis=0,
    )

    rest_far = send_bits(rest_pieces, "high", list(rest_pieces))
    gate_came = send_bits(gate_first, "low", list(gate_first))
    first_near = send_bits(first_pieces, "low", near_all)
    down_theirs = add_along(down_theirs, down_came)
    down_came = send_along(down_mine)
    down_team = swap(down_theirs, "team", 1)
    wide_shape = outer + (rows, -1)
    d_all, d_taps = run_backward(
        place,
        pre,
        d_outs.reshape(wide_shape),
        d_gate_pre.reshape(wide_shape),
        beta_pre,
        cols,
        rows_g,
        taps,
        fresh,
        starts,
        solved,
    )
    groups[:] = []
    small_base, mixer_terms, d_all, d_taps, down_mine, down_came, down_team, gate_came, rest_far, first_near = settle(
        small_base, mixer_terms, d_all, d_taps, down_mine, down_came, down_team, gate_came, rest_far, first_near
    )
    d_all = d_all.reshape(2 * length, -1)

    gate_later = {o: gate_pack(at) for at, o in enumerate(offsets) if not all(o)}
    gate_near = send_bits(gate_later, "low", near_all)
    gate_pieces = add_bits({**gate_first, **gate_later}, gate_came)
    gate_far = {
        o: swap(piece[:value_part], "high", o[0]) for o, piece in gate_pieces.items() if o[0]
    }
    d_all = after(d_all, *[piece for o, piece in gate_pieces.items() if o[0]])
    def taps_of(start, part):
        return d_taps[:KERNEL, start : start + count * part].reshape(KERNEL, count, part)

    taps_rows = jnp.concatenate(
        [
            taps_of(0, key_part),
            taps_of(key_here, key_part),
            taps_of(2 * key_here, value_part),
        ],
        axis=2,
    ).transpose(1, 0, 2)
    taps_rows = jnp.pad(taps_rows, ((0, 0), (0, 16 - KERNEL), (0, model - taps_wide)))
    taps_rows = taps_rows.reshape(count * 16, model).astype(BF16)
    mix_low = run_weigh(d_all, normed, taps_rows, (count, key_part, value_part))
    piece_rows = 2 * key_part + value_part + 16
    beta_term = mix_low[count * piece_rows : count * piece_rows + heads].astype(F32)

    def mix_pack(at):
        return cut(mix_low, at, piece_rows)

    groups[:] = [gate_pieces]
    d_all, gate_far, gate_near, mix_low, d_taps, down_mine, down_came, down_team = settle(
        d_all, gate_far, gate_near, mix_low, d_taps, down_mine, down_came, down_team
    )
    mix_sent = {o: mix_pack(at) for at, o in enumerate(offsets) if all(o)}

    def part_of(pieces, start, stop):
        return {o: piece[start:stop] for o, piece in pieces.items()}

    out_pieces = {o: piece[value_part:] for o, piece in gate_pieces.items() if o[0]}
    out_half = value_part // 32 * 16
    mix_half = (2 * key_part + value_part + 16) // 32 * 16
    out_far = send_bits(part_of(out_pieces, 0, out_half), "high", list(out_pieces))
    mix_came = send_bits(part_of(mix_sent, 0, mix_half), "low", list(mix_sent))
    normed_other, gain_other = run_back(d_all, all_rows, normed, 1)
    d_all, normed_other, gain_other, out_far, mix_came, out_pieces, mix_sent = settle(
        d_all, normed_other, gain_other, out_far, mix_came, out_pieces, mix_sent
    )
    out_next = send_bits(part_of(out_pieces, out_half, None), "high", list(out_pieces))
    mix_next = send_bits(part_of(mix_sent, mix_half, None), "low", list(mix_sent))
    came_other = swap(normed_other, "seq", 1)
    normed_own, gain_own = run_back(d_all, all_rows, normed, 0)
    groups[:] = [gate_pieces, first_pieces, rest_pieces]
    (
        normed_own,
        gain_own,
        came_other,
        out_next,
        mix_next,
        gain_other,
        down_mine,
        down_came,
        down_team,
        beta_term,
        mix_low,
    ) = settle(
        normed_own,
        gain_own,
        came_other,
        out_next,
        mix_next,
        gain_other,
        down_mine,
        down_came,
        down_team,
        beta_term,
        mix_low,
    )
    mix_came = {o: jnp.concatenate([mix_came[o], mix_next[o]], axis=0) for o in mix_came}
    theirs, _ = fold_came(normed_own, came_other)
    mixer_gain_term = (gain_own[0] + gain_other[0]) / (gain_f * gain_f)
    row_ids = lax.broadcasted_iota(jnp.int32, (H + 8, model), 0)
    small_rows = jnp.where(row_ids == H, mixer_gain_term[None], small_base)
    for head in range(heads):
        small_rows = jnp.where(row_ids == head_places[head], beta_term[head][None], small_rows)
    blocks = model // (low_count * gain_part)
    small_terms = small_rows.reshape(H + 8, blocks, -1).transpose(1, 0, 2)
    small_terms = small_terms.reshape(pieces_x, 2, high_count, 2, H + 8, -1)
    groups[:] = []
    theirs_sent = {at: piece for at, piece in theirs.items() if at}
    theirs_sent, normed_own, came_other, small_terms, mix_came, mix_sent, mix_low = settle(
        theirs_sent, normed_own, came_other, small_terms, mix_came, mix_sent, mix_low
    )

    mix_pieces = {
        o: mix_sent[o] if o in mix_sent else mix_pack(at) for at, o in enumerate(offsets)
    }
    mix_pieces = add_bits(mix_pieces, mix_came)
    groups[:] = [mix_pieces, gate_pieces, first_pieces, rest_pieces]
    theirs, mine = fold_came(normed_own, came_other)
    theirs.update(theirs_sent)
    came = send_along(theirs)
    mix_far = {
        o: swap(piece[: 2 * key_part], "high", o[0]) for o, piece in mix_pieces.items() if o[0]
    }
    mix_near = send_bits(mix_pieces, "low", near_all)
    small_terms = sum_stage(small_terms, "team", 3)
    small_terms = sum_stage(small_terms, "seq", 1, (1,))
    small_terms = sum_stage(small_terms, "high", 2)
    theirs, mine, came, small_terms, mix_far, mix_near, first_near, rest_near, rest_far = settle(
        theirs, mine, came, small_terms, mix_far, mix_near, first_near, rest_near, rest_far
    )

    theirs = add_along(theirs, came)
    came_team = swap(theirs, "team", 1)
    small_terms = sum_stage(small_terms, "seq", 0, bits_of(seq_count)[1:])
    came = send_along({at: after(piece, small_terms) for at, piece in mine.items()})
    for bit in bits_of(low_count):
        small_terms = small_terms + swap(small_terms, "low", bit)
    value_far = {
        o: swap(piece[2 * key_part :], "high", o[0]) for o, piece in mix_pieces.items() if o[0]
    }
    given = []

    def known(piece):
        for at, other in enumerate(given):
            if other is piece:
                return at
        given.append(piece)
        return len(given) - 1

    def segment(size, start, pieces, parts=()):
        sources = [(known(piece), start) for piece in pieces]
        for begin, more in parts:
            sources += [(known(piece), start - begin) for piece in more]
        return size, sources

    def spans(start, size, cut_at):
        if start < cut_at < start + size:
            return [(start, cut_at - start), (cut_at, start + size - cut_at)]
        return [(start, size)]

    mix_all = [mix_pieces[0, 0], *mix_near.values()]
    gate_all = [gate_pieces[0, 0], *gate_near.values()]
    first_all = [first_pieces[0, 0], *first_near.values()]
    rest_all = [rest_pieces[0, 0], *rest_near.values(), *rest_far.values()]
    outputs = [
        ([segment(key_part, 0, mix_all + list(mix_far.values()))], False),
        ([segment(key_part, key_part, mix_all + list(mix_far.values()))], False),
        ([segment(value_part, 0, gate_all + list(gate_far.values()))], True),
        (
            [
                segment(
                    size,
                    start,
                    gate_all,
                    [
                        (value_part, out_far.values())
                        if start < value_part + out_half
                        else (value_part + out_half, out_next.values())
                    ],
                )
                for start, size in spans(value_part, value_part, value_part + out_half)
            ],
            False,
        ),
    ]
    for kind in range(3):
        segments = [
            segment(
                size,
                start,
                first_all,
                [(0, first_far.values()) if start < first_half else (first_half, next_far.values())],
            )
            for start, size in spans(kind * first_count, first_count, first_half)
        ]
        segments.append(segment(rest_count, kind * rest_count, rest_all))
        outputs.append((segments, False))
    finished = run_finish(given, outputs)
    mine, came, came_team, value_far, small_terms, finished = settle(
        mine, came, came_team, value_far, small_terms, finished
    )
    small_rows = small_terms.reshape(H + 8, low_count, gain_part)
    small_rows = sum(
        jnp.where(low_pos == at, small_rows[:, at], 0.0) for at in range(low_count)
    )
    beta_sum = small_rows[:H].T
    d_source = add_along(mine, came).astype(F32) + came_team.astype(F32)
    unit = source_f * scale_own
    d_norm = scale_own * (d_source - unit * jnp.mean(unit * d_source, axis=-1, keepdims=True))
    tokens_grad = (d_middle + d_norm).astype(BF16)[None]
    block_out = middle + add_along(down_mine, down_came).astype(F32) + down_team.astype(F32)
    block_out = block_out.astype(BF16)[None]

    value_sum = sum(
        [piece[2 * key_part :].astype(F32) for piece in mix_near.values()],
        mix_pieces[0, 0][2 * key_part :].astype(F32),
    )
    value_sum = sum([piece.astype(F32) for piece in value_far.values()], value_sum)
    taps_sum = value_sum[value_part : value_part + KERNEL, :taps_wide]

    return (
        block_out,
        tokens_grad,
        small_rows[H],
        finished[0].T,
        finished[1].T,
        value_sum[:value_part].T,
        beta_sum,
        finished[2],
        taps_sum[:, :key_part],
        taps_sum[:, key_part : 2 * key_part],
        taps_sum[:, 2 * key_part :],
        small_rows[H + 2, :head_part],
        finished[3],
        small_rows[H + 1],
        finished[4].T,
        finished[5].T,
        finished[6],
    )


def solution(mesh):
    in_specs = (
        P(BATCH, "seq", None),
        P(BATCH, None, "seq"),
        P(BATCH, "seq", None),
        P(ALL),
        P(None, ALL),
        P(None, ALL),
        P(None, ALL),
        P(ALL, None),
        P(None, ALL),
        P(None, ALL),
        P(None, ALL),
        P(None, ALL),
        P(ALL),
        P(ALL, None),
        P(ALL),
        P(None, ALL),
        P(None, ALL),
        P(ALL, None),
    )
    out_specs = (
        P(BATCH, "seq", None),
        P(BATCH, "seq", None),
        P(ALL),
        P(None, ALL),
        P(None, ALL),
        P(None, ALL),
        P(ALL, None),
        P(None, ALL),
        P(None, ALL),
        P(None, ALL),
        P(None, ALL),
        P(ALL),
        P(ALL, None),
        P(ALL),
        P(None, ALL),
        P(None, ALL),
        P(ALL, None),
    )
    seq_count, batch_count = mesh.shape["seq"], mesh.shape["batch"]
    team = seq_count * batch_count // H
    split = mesh.devices.reshape(seq_count, batch_count // (2 * team), 2, team)
    mesh = Mesh(split, ("seq", "high", "team", "low"))
    return jax.shard_map(local, mesh=mesh, in_specs=in_specs, out_specs=out_specs, check_vma=False)
```
